128 devices in a mesh: ctx: 16 (over y_lo, x, core), chan: 8 (over z, y_hi).
Axes of the slice: x: 4, y: 4 (y_hi: 2, y_lo: 2; y = y_hi * 2 + y_lo), z: 4, core: 2. Of those that a mesh axis runs over, the one named last changes fastest.
Arguments:
- feats_se: bfloat16 [3, 4096, 8192], P(None, 'ctx', 'chan'), may hold values from -6 to 6
- filt_se: float32 [512, 7], P('chan'), may hold values from -2.4 to 2.4
- w_out: bfloat16 [8192, 8192], P('chan', 'ctx'), may hold values from -0.0625 to 0.0625
- feats_mr: bfloat16 [2, 4096, 8192], P(None, 'ctx', 'chan'), may hold values from -6 to 6
- filt_mr: float32 [512, 128], P('chan')
- lengths: int32 [8], replicated, may hold values from 1 to 1024, 4096 in all
- owners: int32 [8], replicated, may hold values from 0 to 15, as said below
Outputs:
- mixed: bfloat16 [4096, 8192], P('ctx', 'chan')
- se_state: bfloat16 [16, 6, 8192], P('ctx', None, 'chan')
- mr_state: bfloat16 [16, 127, 8192], P('ctx', None, 'chan')
The draws below stay inside these ranges and needn't reach their ends.
Inputs may be any that keep to these rules, and one draw needn't show every extreme that they name: `lengths`: every request has at least one position; together they fill all 4096 positions, and one is exactly 1024 long. The owners are distinct; 0 and 15 are always among them.
All inputs are finite; a program needn't handle non-finite values.
Results may differ from the reference program's by a relative error of at most 0.018.
Values may be sent and summed in bfloat16 or wider, within the bound.
A program may use at most 128 MiB of HBM per device.

```python
import math
import jax
import jax.numpy as jnp
import numpy as np
from jax import lax

D = 8192
GROUP = 16
SE_TAPS = 7
MR_TAPS = 128
TOK_DEV = 256
TOKENS = 4096
GROUPS = 512
REQUESTS = 8
N_CTX = 16
N_CHAN = 8


def draw_filt_mr(key, part):
    key = jax.random.fold_in(key, 11)
    key_taps, key_rates = jax.random.split(key)
    group_count = D // GROUP
    taps = jnp.arange(MR_TAPS, dtype=jnp.float32)
    noise = jax.random.normal(key_taps, (group_count, MR_TAPS), jnp.float32)
    rates = jnp.exp(jax.random.uniform(key_rates, (group_count, 1), jnp.float32, math.log(0.5 / MR_TAPS), math.log(0.08)))
    return noise * jnp.exp(-rates * taps[None, :]) * (1.5 / MR_TAPS ** 0.5)


def draw_owners(key, part):
    key = jax.random.fold_in(key, 23)
    key_pick, key_order = jax.random.split(key)
    middle = jax.random.permutation(key_pick, N_CTX - 2) + 1
    chosen = jnp.concatenate([jnp.array([0, N_CTX - 1], jnp.int32), middle[:REQUESTS - 2].astype(jnp.int32)])
    return jax.random.permutation(key_order, chosen).astype(jnp.int32)


def block_levels(own_key, extent, cuts, least, high):
    gain = 1.0
    for axis_at, shards_of in cuts:
        heights = jax.random.uniform(jax.random.fold_in(jax.random.fold_in(own_key, 6), axis_at), (shards_of,), jnp.float32, least / len(cuts), high / len(cuts))
        gain = gain * jnp.repeat(jnp.exp(heights), extent[axis_at] // shards_of).reshape((-1,) + (1,) * (len(extent) - 1 - axis_at))
    return gain


def profile(number_of, total, bound, skew):
    portions = [(1 << 20) // math.isqrt(grade ** skew) + 1 for grade in range(2, number_of + 1)]
    rest, holding = total - bound - (number_of - 1), [1] * (number_of - 1)
    while rest > 0:
        candidates = [i for i in range(number_of - 1) if holding[i] < bound]
        whole, remaining = sum([portions[i] for i in candidates]), rest
        for i in candidates:
            extra = min(bound - holding[i], max(1, remaining * portions[i] // whole), rest)
            holding[i] = holding[i] + extra
            rest = rest - extra
    return np.array([bound] + holding)


def ragged_sizes(rng, amount, total, reach, slope):
    if amount == 2:
        one = jax.random.randint(rng, (), max(1, total - reach), min(reach, total - 1) + 1)
        return jnp.stack([one, total - one])
    sizes = jnp.asarray(profile(amount, total, reach, slope), jnp.int32)
    twos = (amount - 1) // 2
    giver, sink = sizes[1:1 + 2 * twos:2], sizes[2:2 + 2 * twos:2]
    slack = jnp.minimum(giver - 1, reach - sink)
    moved = jax.random.randint(jax.random.fold_in(rng, 1), (twos,), 0, 1 << 20) % (slack + 1)
    sizes = sizes.at[1:1 + 2 * twos:2].set(giver - moved).at[2:2 + 2 * twos:2].set(sink + moved)
    return sizes[jax.random.permutation(jax.random.fold_in(rng, 2), amount)]


def normal_values(key, extent, spread, bound, shards=(), kind=jnp.bfloat16):
    entries = jax.random.normal(key, extent, jnp.float32) * spread
    if len(shards) > 0:
        entries = block_levels(key, extent, shards, -0.22, 0.18) * entries
    return jnp.clip(entries, min=-bound, max=bound).astype(kind)


def setup_inputs(seed: int = 0) -> dict:
    streams_of = jax.random.split(jax.random.key(seed), 8)
    feats_se = normal_values(streams_of[0], (3, TOKENS, D), 1.0, 6.0, ((1, 16), (2, 8)))
    filt_se = normal_values(streams_of[1], (GROUPS, SE_TAPS), 0.4, 2.4, ((0, 8),), jnp.float32)
    w_out = normal_values(streams_of[2], (D, D), D ** -0.5, 0.0625, ((0, 8), (1, 16)))
    feats_mr = normal_values(streams_of[3], (2, TOKENS, D), 1.0, 6.0, ((1, 16), (2, 8)))
    filt_mr = draw_filt_mr(jax.random.fold_in(streams_of[7], 71), 0)
    lengths = ragged_sizes(streams_of[5], REQUESTS, TOKENS, 4 * TOK_DEV, 2).astype(jnp.int32)
    owners = draw_owners(jax.random.fold_in(streams_of[7], 71), 0)
    return dict(feats_se=feats_se, filt_se=filt_se, w_out=w_out, feats_mr=feats_mr, filt_mr=filt_mr, lengths=lengths, owners=owners)


def segment_start(starts, positions):
    hit = starts[None, :] <= positions[:, None]
    return jnp.max(jnp.where(hit, starts[None, :], 0), axis=1).astype(jnp.int32)


def toeplitz(filters, block):
    out_step = jnp.arange(block, dtype=jnp.int32)[:, None]
    in_step = jnp.arange(2 * block - 1, dtype=jnp.int32)[None, :]
    delay = out_step + block - 1 - in_step
    valid = (delay >= 0) & (delay < block)
    taken = jnp.take(filters, jnp.clip(delay, 0, block - 1), axis=1)
    return jnp.where(valid[None], taken, jnp.float32(0.0))


def short_conv(padded_input, filt_chan, seg, positions):
    taps = filt_chan.shape[1]
    row_count = positions.shape[0]
    total = jnp.zeros((row_count, padded_input.shape[1]), jnp.float32)
    for delay in range(taps):
        keep = (positions - delay >= seg)[:, None]
        shifted = padded_input[taps - 1 - delay: taps - 1 - delay + row_count]
        total = total + jnp.where(keep, filt_chan[:, delay][None, :] * shifted, jnp.float32(0.0))
    return total


def long_conv(padded_input, filters, seg, first_row):
    block = filters.shape[1]
    row_count = padded_input.shape[0] - block + 1
    group_count = filters.shape[0]
    chan_count = padded_input.shape[1]
    group_width = chan_count // group_count
    table = toeplitz(filters, block)

    def one_block(block_index):
        window = lax.dynamic_slice_in_dim(padded_input, block_index * block, 2 * block - 1, 0)
        window = window.reshape(2 * block - 1, group_count, group_width)
        in_pos = first_row + block_index * block - (block - 1) + jnp.arange(2 * block - 1, dtype=jnp.int32)
        seg_block = lax.dynamic_slice_in_dim(seg, block_index * block, block, 0)
        keep = (in_pos[None, :] >= seg_block[:, None]).astype(jnp.float32)
        out = jnp.einsum('gts,sgc->tgc', table * keep[None], window, precision=lax.Precision.HIGHEST)
        return out.reshape(block, chan_count)

    blocks = lax.map(one_block, jnp.arange(row_count // block, dtype=jnp.int32))
    return blocks.reshape(row_count, chan_count)


def tail_rows(padded_input, ends, starts, span, offset):
    def take_one(end_pos):
        return lax.dynamic_slice_in_dim(padded_input, (end_pos - offset).astype(jnp.int32), span, 0)
    slices = jax.vmap(take_one)(ends)
    pos = ends[:, None] - span + jnp.arange(span, dtype=jnp.int32)[None, :]
    valid = pos >= starts[:, None]
    return jnp.where(valid[:, :, None], slices, jnp.float32(0.0)).astype(jnp.bfloat16)


def reference(feats_se, filt_se, w_out, feats_mr, filt_mr, lengths, owners):
    ends = jnp.cumsum(lengths).astype(jnp.int32)
    starts = (ends - lengths).astype(jnp.int32)
    positions = jnp.arange(TOKENS, dtype=jnp.int32)
    seg = segment_start(starts, positions)
    short_span = SE_TAPS - 1
    long_span = MR_TAPS - 1

    se_in = feats_se[1].astype(jnp.float32) * feats_se[2].astype(jnp.float32)
    se_pad = jnp.concatenate([jnp.zeros((short_span, D), jnp.float32), se_in], axis=0)
    filt_chan = jnp.repeat(filt_se, GROUP, axis=0)
    se_conv = short_conv(se_pad, filt_chan, seg, positions)
    gated = (feats_se[0].astype(jnp.float32) * se_conv).astype(jnp.bfloat16)

    chan_block = D // N_CHAN
    total = jnp.zeros((TOKENS, D), jnp.float32)
    for block_index in range(N_CHAN):
        partial_sum = jnp.dot(gated[:, block_index * chan_block:(block_index + 1) * chan_block],
                              w_out[block_index * chan_block:(block_index + 1) * chan_block],
                              preferred_element_type=jnp.float32)
        rounded = lax.optimization_barrier(partial_sum.astype(jnp.bfloat16))
        total = total + rounded.astype(jnp.float32)
    projected = total.astype(jnp.bfloat16)

    mr_in = feats_mr[1].astype(jnp.float32) * projected.astype(jnp.float32)
    mr_pad = jnp.concatenate([jnp.zeros((long_span, D), jnp.float32), mr_in], axis=0)
    mr_conv = long_conv(mr_pad, filt_mr, seg, jnp.int32(0))
    mixed = (feats_mr[0].astype(jnp.float32) * mr_conv).astype(jnp.bfloat16)

    target = owners.astype(jnp.int32)
    se_tails = tail_rows(se_pad, ends, starts, short_span, 0)
    mr_tails = tail_rows(mr_pad, ends, starts, long_span, 0)
    se_state = jnp.zeros((N_CTX, short_span, D), jnp.bfloat16).at[target].set(se_tails)
    mr_state = jnp.zeros((N_CTX, long_span, D), jnp.bfloat16).at[target].set(mr_tails)
    return mixed, se_state, mr_state
```

```python
import jax
import jax.numpy as jnp
from jax import lax
from jax.experimental import pallas as pl
from jax.experimental.pallas import tpu as pltpu
from jax.sharding import PartitionSpec as P

BF16, F32, I32 = jnp.bfloat16, jnp.float32, jnp.int32
MESH = pl.DeviceIdType.MESH
ROWS, WIDTH, LANES = 256, 1024, 128
TAPS, SPAN = 7, 128
FAR = 1 << 20


def iota(shape, axis):
    return lax.broadcasted_iota(I32, shape, axis)


def kernel(
    lengths, owners, filt_se, filt_mr, feats_se, w_out, feats_mr,
    mixed, se_state, mr_state,
    feat, halo, gates, se_in, rel, wq, wbuf, abuf, cstage, zbuf, red, proj, g0, toep,
    xh, xe, slot, slot_in, se_bf, se_part, se_pin, se_slot, se_sin, big, taps,
    load_sem, halo_sem, ws_s, ws_r, xs_s, xs_r, rl_s, rl_r, as_s, as_r, ar_s, ar_r, cf_s, cf_r,
    zs_s, zs_r, fs_s, fs_r, mx_s, mx_r, st_s, st_r, sp_s, sp_r, sq_s, sq_r,
):
    ctx, chan = lax.axis_index("ctx"), lax.axis_index("chan")
    core, x, low = lax.rem(ctx, 2), lax.rem(lax.div(ctx, 2), 4), lax.div(ctx, 8)
    high, z = lax.rem(chan, 2), lax.div(chan, 2)
    y = high * 2 + low

    def device(px, py, pz, pc):
        return {"ctx": lax.rem(py, 2) * 8 + px * 2 + pc, "chan": pz * 2 + lax.div(py, 2)}

    def near(dx, dy, dz, dc):
        return device(lax.rem(x + dx, 4), lax.rem(y + dy, 4), lax.rem(z + dz, 4), lax.rem(core + dc, 2))

    other = near(0, 0, 0, 1)
    partner = device(x, high * 2 + 1 - low, z, core)
    across = device(x, high * 2 + 1 - low, z, 1 - core)
    after, before = {"ctx": lax.rem(ctx + 1, 16)}, {"ctx": lax.rem(ctx + 15, 16)}

    def remote(src, dst, send, recv, to):
        return pltpu.make_async_remote_copy(
            src_ref=src, dst_ref=dst, send_sem=send, recv_sem=recv, device_id=to, device_id_type=MESH
        )

    sent = []

    def push(src, dst, send, recv, to):
        copy = remote(src, dst, send, recv, to)
        copy.start()
        sent.append(copy)

    def arrived(ref, recv):
        remote(ref, ref, recv, recv, other).wait_recv()

    def load(src, dst, at):
        copy = pltpu.make_async_copy(src, dst, load_sem.at[at])
        copy.start()
        return copy

    w_loads = []
    for dy in range(4):
        q = lax.rem(y + dy, 4)
        src = w_out.at[:, pl.ds(pl.multiple_of(q * LANES, LANES), LANES)]
        w_loads.append(load(src, wbuf.at[0, y] if dy == 0 else wq.at[dy - 1], dy))
    kv_load = load(feats_se.at[pl.ds(1, 2)], feat.at[pl.ds(1, 2)], 4)
    q_load = load(feats_se.at[0], feat.at[0], 5)
    mr_load = load(feats_mr, gates, 6)

    barrier = pltpu.get_barrier_semaphore()
    peers = [after, before]
    peers += [near(0, dy, 0, dc) for dy in range(4) for dc in range(2) if dy or dc]
    peers += [near(d, 0, 0, 0) for d in (1, 2, 3)] + [near(0, 0, d, 0) for d in (1, 2, 3)]
    for peer in peers:
        pl.semaphore_signal(barrier, inc=1, device_id=peer, device_id_type=MESH)
    pl.semaphore_wait(barrier, len(peers))

    kv_load.wait()
    push(feat.at[pl.ds(1, 2), pl.ds(ROWS - 16, 16)], halo, halo_sem.at[0], halo_sem.at[1], after)
    for dy in (1, 3, 2):
        w_loads[dy].wait()
        push(wq.at[dy - 1], wbuf.at[0, y], ws_s.at[dy - 1], ws_r.at[dy - 1], near(0, dy, 0, 0))
    w_loads[0].wait()

    order = [y, lax.rem(y + 3, 4), lax.rem(y + 1, 4), lax.rem(y + 2, 4)]

    def spread(k):
        if k:
            arrived(wbuf.at[0, order[k]], ws_r.at[(0, 1, 3, 2)[k] - 1])
        push(wbuf.at[0, order[k]], wbuf.at[3, order[k]], xs_s.at[0, k], xs_r.at[0, k], near(1, 0, 0, 0))
        push(wbuf.at[0, order[k]], wbuf.at[1, order[k]], xs_s.at[1, k], xs_r.at[1, k], near(3, 0, 0, 0))

    def pass_on(k):
        half = WIDTH // 2
        first, second = pl.ds(0, half), pl.ds(half, half)
        arrived(wbuf.at[3, order[k]], xs_r.at[0, k])
        push(wbuf.at[3, order[k], first], wbuf.at[2, order[k], first], rl_s.at[0, k], rl_r.at[0, k], near(1, 0, 0, 0))
        arrived(wbuf.at[1, order[k]], xs_r.at[1, k])
        push(wbuf.at[1, order[k], second], wbuf.at[2, order[k], second], rl_s.at[1, k], rl_r.at[1, k], near(3, 0, 0, 0))

    def passed(k):
        half = WIDTH // 2
        arrived(wbuf.at[2, order[k], pl.ds(0, half)], rl_r.at[0, k])
        arrived(wbuf.at[2, order[k], pl.ds(half, half)], rl_r.at[1, k])

    spread(0)

    starts, ends = [], []
    total = jnp.int32(0)
    for r in range(8):
        starts.append(total)
        total = total + lengths[r]
        ends.append(total)
    pos = iota((ROWS, LANES), 0) + ctx * ROWS
    seg = jnp.zeros((ROWS, LANES), I32)
    for r in range(8):
        seg = jnp.maximum(seg, jnp.where(starts[r] <= pos, starts[r], 0))
    rel[...] = pos - seg

    spread_out = jnp.where(lax.div(iota((64, WIDTH), 1), 16) == iota((64, WIDTH), 0), 1.0, 0.0).astype(F32)
    taps[pl.ds(0, TAPS), :] = lax.dot_general(
        filt_se[...], spread_out, (((0,), (0,)), ((), ())),
        precision=lax.Precision.HIGHEST, preferred_element_type=F32,
    )
    se_in[pl.ds(16, ROWS), :] = feat[1].astype(F32) * feat[2].astype(F32)
    se_bf[...] = se_in[pl.ds(16, ROWS), :].astype(BF16)
    q_load.wait()
    arrived(halo, halo_sem.at[1])
    se_in[pl.ds(0, 16), :] = halo[0].astype(F32) * halo[1].astype(F32)

    @pl.loop(0, WIDTH // LANES)
    def _(p):
        lanes = pl.ds(pl.multiple_of(p * LANES, LANES), LANES)
        acc = jnp.zeros((ROWS, LANES), F32)
        for j in range(TAPS):
            term = taps[pl.ds(j, 1), lanes] * se_in[pl.ds(16 - j, ROWS), lanes]
            acc = acc + jnp.where(rel[...] >= j, term, 0.0)
        abuf[y, core, :, lanes] = (feat[0, :, lanes].astype(F32) * acc).astype(BF16)

    mine = abuf.at[y, core]
    push(mine, mine, as_s.at[0], as_r.at[0], near(0, 1, 0, 0))
    push(mine, mine, as_s.at[1], as_r.at[1], near(0, 3, 0, 0))
    push(mine, mine, cf_s.at[0], cf_r.at[0], other)

    def request_at(target):
        end = jnp.int32(-FAR)
        start = jnp.int32(0)
        for r in range(8):
            end = jnp.where(owners[r] == target, ends[r], end)
            start = jnp.where(owners[r] == target, starts[r], start)
        return end, start

    def picker(target, base, span, rows):
        end, start = request_at(target)
        at = iota((rows, ROWS), 1) + base
        row = iota((rows, ROWS), 0)
        keep = (at == end - span + row) & (at >= start) & (row < span)
        return jnp.where(keep, 1.0, 0.0).astype(BF16)

    groups = [(low, core), (low, 1 - core), (1 - low, core), (1 - low, 1 - core)]
    for g, (to_low, to_core) in enumerate(groups):
        rows = [
            picker(to_low * 8 + lax.rem(x + r, 4) * 2 + to_core, ctx * ROWS, TAPS - 1, 16) for r in range(4)
        ]
        se_part[g] = jnp.dot(
            jnp.concatenate(rows, axis=0), se_bf[...], preferred_element_type=F32
        ).astype(BF16)
    for g, to in ((1, other), (2, partner), (3, across)):
        push(se_part.at[g], se_pin.at[g], sp_s.at[g], sp_r.at[g], to)

    spread(1)
    spread(2)

    turn = jnp.where(lax.rem(iota((SPAN, SPAN), 0) + iota((SPAN, SPAN), 1), SPAN) == 0, 1.0, 0.0)
    g0[...] = jnp.dot(filt_mr[...].astype(BF16), turn.astype(BF16), preferred_element_type=F32)

    def band(first, count):
        @pl.loop(first, first + count)
        def _(g):
            ring = pltpu.roll(
                jnp.broadcast_to(g0[pl.ds(g, 1), :], (SPAN, SPAN)), 0, 1, stride=1, stride_axis=0
            )
            step = iota((SPAN, SPAN), 0) - iota((SPAN, SPAN), 1)
            for b in range(2):
                reach = rel[pl.ds(b * SPAN, SPAN), :]
                left = jnp.where((step < 0) & (step + SPAN <= reach), ring, 0.0)
                right = jnp.where((step >= 0) & (step <= reach), ring, 0.0)
                toep[b, g, :, pl.ds(0, SPAN)] = left.astype(BF16)
                toep[b, g, :, pl.ds(SPAN, SPAN)] = right.astype(BF16)

    band(0, 32)
    spread(3)
    band(32, 32)

    half = pl.ds(0, ROWS // 2), pl.ds(ROWS // 2, ROWS // 2)
    down, up, far = order[1], order[2], order[3]
    arrived(abuf.at[down, core], as_r.at[0])
    push(abuf.at[down, core, half[0]], abuf.at[down, core, half[0]], ar_s.at[0], ar_r.at[0], near(0, 1, 0, 0))
    push(abuf.at[down, core], abuf.at[down, core], cf_s.at[1], cf_r.at[1], other)
    arrived(abuf.at[up, core], as_r.at[1])
    push(abuf.at[up, core, half[1]], abuf.at[up, core, half[1]], ar_s.at[1], ar_r.at[1], near(0, 3, 0, 0))
    push(abuf.at[up, core], abuf.at[up, core], cf_s.at[2], cf_r.at[2], other)

    for g in (1, 2, 3):
        arrived(se_pin.at[g], sp_r.at[g])
    se_slot[...] = (
        se_part[0].astype(F32) + se_pin[1].astype(F32) + se_pin[2].astype(F32) + se_pin[3].astype(F32)
    ).astype(BF16)
    for r in (1, 2, 3):
        push(se_slot.at[pl.ds(16 * r, 16)], se_sin.at[r], sq_s.at[r], sq_r.at[r], near(r, 0, 0, 0))

    pass_on(0)
    pass_on(1)

    z_sends = []

    def task(tl, r):
        token_low = low if tl == 0 else 1 - low

        @pl.loop(0, 2)
        def _(cc):
            acc = None
            for hh in range(2):
                right = jnp.concatenate([wbuf[r, 2 * hh], wbuf[r, 2 * hh + 1]], axis=1)
                part = jnp.dot(abuf[2 * hh + token_low, cc], right, preferred_element_type=F32)
                acc = part if acc is None else acc + part
            rows = pl.ds(pl.multiple_of(cc * ROWS, ROWS), ROWS)
            cstage[tl, r, 0, rows, :] = acc[:, :LANES].astype(BF16)
            cstage[tl, r, 1, rows, :] = acc[:, LANES:].astype(BF16)

        px = lax.rem(x + r, 4)
        e = lax.rem(px, 2)
        for ll in range(2):
            pz = 2 * ll + lax.div(px, 2)
            dz = lax.rem(pz - z + 4, 4)
            copy = remote(
                cstage.at[tl, r, ll], zbuf.at[dz, tl, e], zs_s.at[tl, r, ll], zs_r.at[dz, tl, e],
                device(x, y, pz, core),
            )
            z_sends.append((dz, copy))

            @pl.when(dz > 0)
            def _():
                copy.start()

    arrived(abuf.at[y, 1 - core], cf_r.at[0])
    arrived(abuf.at[down, 1 - core], cf_r.at[1])
    arrived(abuf.at[up, 1 - core], cf_r.at[2])
    task(1, 0)
    pass_on(2)
    pass_on(3)
    task(1, 1)
    task(1, 3)
    arrived(abuf.at[far, core, half[0]], ar_r.at[0])
    arrived(abuf.at[far, core, half[1]], ar_r.at[1])
    push(abuf.at[far, core], abuf.at[far, core], cf_s.at[3], cf_r.at[3], other)
    arrived(abuf.at[far, 1 - core], cf_r.at[3])
    task(0, 0)
    task(0, 1)
    task(0, 3)
    for k in range(4):
        passed(k)
    task(1, 2)
    task(0, 2)

    own_x = lax.rem(z, 2) * 2
    for tl in (1, 0):
        for e in range(2):
            total = cstage[tl, lax.rem(own_x + e - x + 4, 4), lax.div(z, 2)].astype(F32)
            for dz in (1, 2, 3):
                arrived(zbuf.at[dz, tl, e], zs_r.at[dz, tl, e])
                total = total + zbuf[dz, tl, e].astype(F32)
            red[tl, e] = total.astype(BF16)
        for dy in (2, 0) if tl == 0 else (1, 3):
            for dc in (1, 0):
                e = lax.div(lax.rem(y + dy, 4), 2)
                pc = lax.rem(core + dc, 2)
                rows = pl.ds(pl.multiple_of(pc * ROWS, ROWS), ROWS)
                if dy == 0 and dc == 0:
                    proj[core * 4 + y] = red[tl, e, rows, :]
                else:
                    push(red.at[tl, e, rows], proj.at[core * 4 + y], fs_s.at[dy, dc], fs_r.at[dy, dc], near(0, dy, 0, dc))
    mr_load.wait()
    for dy in range(4):
        for dc in range(2):
            if dy or dc:
                at = lax.rem(core + dc, 2) * 4 + lax.rem(y + 4 - dy, 4)
                arrived(proj.at[at], fs_r.at[dy, dc])

    for p in range(WIDTH // LANES):
        lanes = pl.ds(p * LANES, LANES)
        xh[pl.ds(SPAN, ROWS), lanes] = (gates[1, :, lanes].astype(F32) * proj[p].astype(F32)).astype(BF16)

    own = xh.at[pl.ds(SPAN, ROWS)]
    push(own, xe.at[1], mx_s.at[1], mx_r.at[1], partner)
    push(xh.at[pl.ds(ROWS, SPAN)], xh.at[pl.ds(0, SPAN)], mx_s.at[0], mx_r.at[0], after)
    push(own, xe.at[0], mx_s.at[2], mx_r.at[2], other)

    def convolve(b):
        @pl.loop(0, WIDTH // LANES)
        def _(p):
            lanes = pl.ds(pl.multiple_of(p * LANES, LANES), LANES)
            left = toep[b, pl.ds(p * 8, 8)].reshape(8 * SPAN, 2 * SPAN)
            big[...] = jnp.dot(left, xh[pl.ds(b * SPAN, 2 * SPAN), lanes], preferred_element_type=F32)
            group = lax.div(iota((SPAN, LANES), 1), 16)
            out = big[pl.ds(0, SPAN), :]
            for g in range(1, 8):
                out = jnp.where(group == g, big[pl.ds(g * SPAN, SPAN), :], out)
            rows = pl.ds(b * SPAN, SPAN)
            mixed[rows, lanes] = (gates[0, rows, lanes].astype(F32) * out).astype(BF16)

    convolve(1)
    arrived(xh.at[pl.ds(0, SPAN)], mx_r.at[0])
    convolve(0)

    arrived(xe.at[0], mx_r.at[2])
    arrived(xe.at[1], mx_r.at[1])
    push(xe.at[1], xe.at[2], mx_s.at[3], mx_r.at[3], other)
    arrived(xe.at[2], mx_r.at[3])
    bases = [ctx, ctx + 1 - 2 * core, ctx + 8 - 16 * low, ctx + 8 - 16 * low + 1 - 2 * core]

    for r in (1, 3, 2, 0):
        target = low * 8 + lax.rem(x + r, 4) * 2 + core
        acc = jnp.dot(picker(target, bases[0] * ROWS, SPAN - 1, SPAN), xh[pl.ds(SPAN, ROWS), :], preferred_element_type=F32)
        for i in range(3):
            acc = acc + jnp.dot(
                picker(target, bases[i + 1] * ROWS, SPAN - 1, SPAN), xe[i], preferred_element_type=F32
            )
        slot[r] = acc.astype(BF16)
        if r:
            push(slot.at[r], slot_in.at[r], st_s.at[r], st_r.at[r], near(r, 0, 0, 0))

    se_total = se_slot[pl.ds(0, 16), :].astype(F32)
    for r in (1, 2, 3):
        arrived(se_sin.at[r], sq_r.at[r])
        se_total = se_total + se_sin[r].astype(F32)
    se_state[0] = se_total.astype(BF16)
    for r in (1, 2, 3):
        arrived(slot_in.at[r], st_r.at[r])
    mr_state[0] = (
        slot[0].astype(F32) + slot_in[1].astype(F32) + slot_in[2].astype(F32) + slot_in[3].astype(F32)
    ).astype(BF16)

    for copy in sent:
        copy.wait_send()
    for dz, copy in z_sends:

        @pl.when(dz > 0)
        def _():
            copy.wait_send()


def on_device(feats_se, filt_se, w_out, feats_mr, filt_mr, lengths, owners):
    vmem, smem = pl.BlockSpec(memory_space=pltpu.VMEM), pl.BlockSpec(memory_space=pltpu.SMEM)
    anywhere = pl.BlockSpec(memory_space=pl.ANY)
    dma = pltpu.SemaphoreType.DMA
    scratch = [
        pltpu.VMEM((3, ROWS, WIDTH), BF16),
        pltpu.VMEM((2, 16, WIDTH), BF16),
        pltpu.VMEM((2, ROWS, WIDTH), BF16),
        pltpu.VMEM((ROWS + 16, WIDTH), F32),
        pltpu.VMEM((ROWS, LANES), I32),
        pltpu.VMEM((3, WIDTH, LANES), BF16),
        pltpu.VMEM((4, 4, WIDTH, LANES), BF16),
        pltpu.VMEM((4, 2, ROWS, WIDTH), BF16),
        pltpu.VMEM((2, 4, 2, 2 * ROWS, LANES), BF16),
        pltpu.VMEM((4, 2, 2, 2 * ROWS, LANES), BF16),
        pltpu.VMEM((2, 2, 2 * ROWS, LANES), BF16),
        pltpu.VMEM((8, ROWS, LANES), BF16),
        pltpu.VMEM((64, SPAN), F32),
        pltpu.VMEM((2, 64, SPAN, 2 * SPAN), BF16),
        pltpu.VMEM((ROWS + SPAN, WIDTH), BF16),
        pltpu.VMEM((3, ROWS, WIDTH), BF16),
        pltpu.VMEM((4, SPAN, WIDTH), BF16),
        pltpu.VMEM((4, SPAN, WIDTH), BF16),
        pltpu.VMEM((ROWS, WIDTH), BF16),
        pltpu.VMEM((4, 64, WIDTH), BF16),
        pltpu.VMEM((4, 64, WIDTH), BF16),
        pltpu.VMEM((64, WIDTH), BF16),
        pltpu.VMEM((4, 16, WIDTH), BF16),
        pltpu.VMEM((8 * SPAN, LANES), F32),
        pltpu.VMEM((8, WIDTH), F32),
        dma((7,)), dma((2,)),
        dma((3,)), dma((3,)), dma((2, 4)), dma((2, 4)), dma((2, 4)), dma((2, 4)),
        dma((2,)), dma((2,)), dma((2,)), dma((2,)), dma((4,)), dma((4,)),
        dma((2, 4, 2)), dma((4, 2, 2)), dma((4, 2)), dma((4, 2)),
        dma((4,)), dma((4,)), dma((4,)), dma((4,)), dma((4,)), dma((4,)), dma((4,)), dma((4,)),
    ]
    mixed, se_state, mr_state = pl.pallas_call(
        kernel,
        out_shape=(
            jax.ShapeDtypeStruct((ROWS, WIDTH), BF16),
            jax.ShapeDtypeStruct((1, 16, WIDTH), BF16),
            jax.ShapeDtypeStruct((1, SPAN, WIDTH), BF16),
        ),
        in_specs=[smem, smem, vmem, vmem, anywhere, anywhere, anywhere],
        out_specs=(vmem, vmem, vmem),
        scratch_shapes=scratch,
        compiler_params=pltpu.CompilerParams(
            collective_id=0, has_side_effects=True, vmem_limit_bytes=52 * 2**20
        ),
        cost_estimate=pl.CostEstimate(flops=5 * 10**9, bytes_accessed=5 * 10**6, transcendentals=0),
        name="hyena",
    )(lengths, owners, filt_se, filt_mr, feats_se, w_out, feats_mr)
    return mixed, se_state[:, : TAPS - 1], mr_state[:, : SPAN - 1]


def solution(mesh):
    in_specs = (
        P(None, "ctx", "chan"),
        P("chan", None),
        P("chan", "ctx"),
        P(None, "ctx", "chan"),
        P("chan", None),
        P(),
        P(),
    )
    out_specs = (P("ctx", "chan"), P("ctx", None, "chan"), P("ctx", None, "chan"))
    return jax.shard_map(
        on_device, mesh=mesh, in_specs=in_specs, out_specs=out_specs, check_vma=False
    )
```

```python
import jax
import jax.numpy as jnp
from jax import lax
from jax.experimental import pallas as pl
from jax.experimental.pallas import tpu as pltpu
from jax.sharding import PartitionSpec as P

BF16, F32, I32 = jnp.bfloat16, jnp.float32, jnp.int32
MESH = pl.DeviceIdType.MESH
ROWS, WIDTH, LANES = 256, 1024, 128
TAPS, SPAN = 7, 128
FAR = 1 << 20


def iota(shape, axis):
    return lax.broadcasted_iota(I32, shape, axis)


def kernel(
    lengths_in, owners_in, filt_se_in, filt_mr_in, feats_se, w_out, feats_mr,
    mixed, se_state, mr_state,
    lengths, owners, filt_se, filt_mr,
    feat, halo, gate, kp, kz, se_in, rel, wq, wbuf, abuf, cstage, zbuf, red, g0, toep, pick,
    xh, slot, slot_in, slot_sum, st, se_bf, se_part, se_pin, se_slot, se_sin, big, taps,
    load_sem, halo_sem, ws_s, ws_r, xs_s, xs_r, rl_s, rl_r, as_s, as_r, ar_s, ar_r, cf_s, cf_r,
    k_s, k_r, zs_s, zs_r, fs_s, fs_r, mx_s, mx_r, st_s, st_r, sy_s, sy_r, sp_s, sp_r, sq_s, sq_r,
):
    ctx, chan = lax.axis_index("ctx"), lax.axis_index("chan")
    core, x, low = lax.rem(ctx, 2), lax.rem(lax.div(ctx, 2), 4), lax.div(ctx, 8)
    high, z = lax.rem(chan, 2), lax.div(chan, 2)
    y = high * 2 + low

    def device(px, py, pz, pc):
        return {"ctx": lax.rem(py, 2) * 8 + px * 2 + pc, "chan": pz * 2 + lax.div(py, 2)}

    def near(dx, dy, dz, dc):
        return device(lax.rem(x + dx, 4), lax.rem(y + dy, 4), lax.rem(z + dz, 4), lax.rem(core + dc, 2))

    other = near(0, 0, 0, 1)
    partner = device(x, high * 2 + 1 - low, z, core)
    across = device(x, high * 2 + 1 - low, z, 1 - core)
    after, before = {"ctx": lax.rem(ctx + 1, 16)}, {"ctx": lax.rem(ctx + 15, 16)}

    def remote(src, dst, send, recv, to):
        return pltpu.make_async_remote_copy(
            src_ref=src, dst_ref=dst, send_sem=send, recv_sem=recv, device_id=to, device_id_type=MESH
        )

    sent = []

    def push(src, dst, send, recv, to):
        copy = remote(src, dst, send, recv, to)
        copy.start()
        sent.append(copy)

    def arrived(ref, recv):
        remote(ref, ref, recv, recv, other).wait_recv()

    def load(src, dst, at):
        copy = pltpu.make_async_copy(src, dst, load_sem.at[at])
        copy.start()
        return copy

    def column(q):
        return pl.ds(pl.multiple_of(q * LANES, LANES), LANES)

    w_loads = [None] * 4
    for dy in (1, 3, 2, 0):
        src = w_out.at[:, column(lax.rem(y + dy, 4))]
        w_loads[dy] = load(src, wbuf.at[0, y] if dy == 0 else wq.at[dy - 1], dy)
    kv_load = load(feats_se.at[pl.ds(1, 2)], feat.at[pl.ds(1, 2)], 4)
    small = [load(lengths_in, lengths, 7), load(filt_se_in, filt_se, 9)]
    q_load = load(feats_se.at[0], feat.at[0], 5)
    late = [load(owners_in, owners, 8), load(filt_mr_in, filt_mr, 10)]
    gate_load = load(feats_mr.at[0], gate, 6)
    k_loads = []
    for dy in range(4):
        for dc in range(2):
            p = lax.rem(core + dc, 2) * 4 + lax.rem(y + dy, 4)
            dst = kp.at[dy, dc] if dy or dc else kz.at[high, low, core]
            k_loads.append(load(feats_mr.at[1, :, column(p)], dst, 11 + dy * 2 + dc))

    barrier = pltpu.get_barrier_semaphore()
    peers = [after, before]
    peers += [near(0, dy, 0, dc) for dy in range(4) for dc in range(2) if dy or dc]
    peers += [near(d, 0, 0, 0) for d in (1, 2, 3)] + [near(0, 0, d, 0) for d in (1, 2, 3)]
    for peer in peers:
        pl.semaphore_signal(barrier, inc=1, device_id=peer, device_id_type=MESH)
    pl.semaphore_wait(barrier, len(peers))

    push(feats_se.at[pl.ds(1, 2), pl.ds(ROWS - 16, 16)], halo, halo_sem.at[0], halo_sem.at[1], after)
    for dy in (1, 3, 2):
        w_loads[dy].wait()
        push(wq.at[dy - 1], wbuf.at[0, y], ws_s.at[dy - 1], ws_r.at[dy - 1], near(0, dy, 0, 0))
    w_loads[0].wait()

    order = [y, lax.rem(y + 3, 4), lax.rem(y + 1, 4), lax.rem(y + 2, 4)]
    down, up, far = order[1], order[2], order[3]

    def spread(k):
        if k:
            arrived(wbuf.at[0, order[k]], ws_r.at[(0, 1, 3, 2)[k] - 1])
        push(wbuf.at[0, order[k]], wbuf.at[3, order[k]], xs_s.at[0, k], xs_r.at[0, k], near(1, 0, 0, 0))
        push(wbuf.at[0, order[k]], wbuf.at[1, order[k]], xs_s.at[1, k], xs_r.at[1, k], near(3, 0, 0, 0))

    def pass_on(k):
        half = WIDTH // 2
        first, second = pl.ds(0, half), pl.ds(half, half)
        arrived(wbuf.at[3, order[k]], xs_r.at[0, k])
        push(wbuf.at[3, order[k], first], wbuf.at[2, order[k], first], rl_s.at[0, k], rl_r.at[0, k], near(1, 0, 0, 0))
        arrived(wbuf.at[1, order[k]], xs_r.at[1, k])
        push(wbuf.at[1, order[k], second], wbuf.at[2, order[k], second], rl_s.at[1, k], rl_r.at[1, k], near(3, 0, 0, 0))

    def passed(k):
        half = WIDTH // 2
        arrived(wbuf.at[2, order[k], pl.ds(0, half)], rl_r.at[0, k])
        arrived(wbuf.at[2, order[k], pl.ds(half, half)], rl_r.at[1, k])

    spread(0)

    for copy in small:
        copy.wait()
    starts, ends = [], []
    total = jnp.int32(0)
    for r in range(8):
        starts.append(total)
        total = total + lengths[r]
        ends.append(total)
    pos = iota((ROWS, LANES), 0) + ctx * ROWS
    seg = jnp.zeros((ROWS, LANES), I32)
    for r in range(8):
        seg = jnp.maximum(seg, jnp.where(starts[r] <= pos, starts[r], 0))
    rel[...] = pos - seg

    spread_out = jnp.where(lax.div(iota((64, WIDTH), 1), 16) == iota((64, WIDTH), 0), 1.0, 0.0).astype(F32)
    taps[pl.ds(0, TAPS), :] = lax.dot_general(
        filt_se[...], spread_out, (((1,), (0,)), ((), ())),
        precision=lax.Precision.HIGHEST, preferred_element_type=F32,
    )
    kv_load.wait()
    se_in[pl.ds(16, ROWS), :] = feat[1].astype(F32) * feat[2].astype(F32)
    se_bf[...] = se_in[pl.ds(16, ROWS), :].astype(BF16)
    q_load.wait()

    def short(first, count):
        @pl.loop(0, WIDTH // LANES)
        def _(p):
            lanes = column(p)
            acc = jnp.zeros((count, LANES), F32)
            for j in range(TAPS):
                term = taps[pl.ds(j, 1), lanes] * se_in[pl.ds(16 + first - j, count), lanes]
                acc = acc + jnp.where(rel[pl.ds(first, count), :] >= j, term, 0.0)
            rows = pl.ds(first, count)
            abuf[y, core, rows, lanes] = (feat[0, rows, lanes].astype(F32) * acc).astype(BF16)

    short(16, ROWS - 16)
    arrived(halo, halo_sem.at[1])
    se_in[pl.ds(0, 16), :] = halo[0].astype(F32) * halo[1].astype(F32)
    short(0, 16)

    half = pl.ds(0, ROWS // 2), pl.ds(ROWS // 2, ROWS // 2)
    for i in range(2):
        for way in range(2):
            mine = abuf.at[y, core, half[i ^ way]]
            push(mine, mine, as_s.at[way, i], as_r.at[way, i], near(0, (1, 3)[way], 0, 0))
    mine = abuf.at[y, core]
    push(mine, mine, cf_s.at[0], cf_r.at[0], other)

    for copy in late:
        copy.wait()

    def request_at(target):
        end = jnp.int32(-FAR)
        start = jnp.int32(0)
        for r in range(8):
            end = jnp.where(owners[r] == target, ends[r], end)
            start = jnp.where(owners[r] == target, starts[r], start)
        return end, start

    def picker(end, start, base, span, rows):
        at = iota((rows, ROWS), 1) + base
        row = iota((rows, ROWS), 0)
        keep = (at == end - span + row) & (at >= start) & (row < span)
        return jnp.where(keep, 1.0, 0.0).astype(BF16)

    groups = [(low, core), (low, 1 - core), (1 - low, core), (1 - low, 1 - core)]
    for g, (to_low, to_core) in enumerate(groups):
        rows = []
        for r in range(4):
            end, start = request_at(to_low * 8 + lax.rem(x + r, 4) * 2 + to_core)
            rows.append(picker(end, start, ctx * ROWS, TAPS - 1, 8))
        se_part[g] = jnp.dot(
            jnp.concatenate(rows, axis=0), se_bf[...], preferred_element_type=F32
        ).astype(BF16)

    spread(1)
    spread(2)

    turn = jnp.where(lax.rem(iota((SPAN, SPAN), 0) + iota((SPAN, SPAN), 1), SPAN) == 0, 1.0, 0.0)
    g0[...] = jnp.dot(filt_mr[...].astype(BF16), turn.astype(BF16), preferred_element_type=F32)

    def band(first, count):
        @pl.loop(first, first + count)
        def _(g):
            ring = pltpu.roll(
                jnp.broadcast_to(g0[pl.ds(g, 1), :], (SPAN, SPAN)), 0, 1, stride=1, stride_axis=0
            )
            step = iota((SPAN, SPAN), 0) - iota((SPAN, SPAN), 1)
            for b in range(2):
                reach = rel[pl.ds(b * SPAN, SPAN), :]
                left = jnp.where((step < 0) & (step + SPAN <= reach), ring, 0.0)
                right = jnp.where((step >= 0) & (step <= reach), ring, 0.0)
                toep[b, g, :, pl.ds(0, SPAN)] = left.astype(BF16)
                toep[b, g, :, pl.ds(SPAN, SPAN)] = right.astype(BF16)

    band(0, 24)
    pass_on(0)
    spread(3)
    band(24, 40)

    @pl.loop(0, 16)
    def _(i):
        target = lax.rem(lax.div(i, 2), 2) * 8 + lax.rem(x + lax.div(i, 4), 4) * 2 + lax.rem(i, 2)
        end, start = request_at(target)
        for b in range(4):
            base = ((b // 2) * 8 + x * 2 + b % 2) * ROWS
            pick[i, :, pl.ds(b * ROWS, ROWS)] = picker(end, start, base, SPAN - 1, SPAN)

    pass_on(1)
    pass_on(2)
    def to_core(block, part, at):
        push(abuf.at[block, core, part], abuf.at[block, core, part], cf_s.at[at], cf_r.at[at], other)

    arrived(abuf.at[down, core, half[0]], as_r.at[0, 0])
    push(abuf.at[down, core, half[0]], abuf.at[down, core, half[0]], ar_s.at[0], ar_r.at[0], near(0, 1, 0, 0))
    to_core(down, half[0], 1)
    arrived(abuf.at[up, core, half[1]], as_r.at[1, 0])
    push(abuf.at[up, core, half[1]], abuf.at[up, core, half[1]], ar_s.at[1], ar_r.at[1], near(0, 3, 0, 0))
    to_core(up, half[1], 2)
    arrived(abuf.at[down, core, half[1]], as_r.at[0, 1])
    to_core(down, half[1], 3)
    arrived(abuf.at[up, core, half[0]], as_r.at[1, 1])
    to_core(up, half[0], 4)

    z_sends = []

    def send_part(tl, r, ll):
        px = lax.rem(x + r, 4)
        pz = 2 * ll + lax.div(px, 2)
        dz = lax.rem(pz - z + 4, 4)
        e = lax.rem(px, 2)
        copy = remote(
            cstage.at[tl, r, ll], zbuf.at[dz, tl, e], zs_s.at[tl, r, ll], zs_r.at[dz, tl, e],
            device(x, y, pz, core),
        )
        z_sends.append((dz, copy))

        @pl.when(dz > 0)
        def _():
            copy.start()

    def task(tl, r, half_of=None):
        token_low = low if tl == 0 else 1 - low

        @pl.loop(0, 2)
        def _(cc):
            acc = None
            for hh in range(2):
                if half_of is None:
                    right = jnp.concatenate([wbuf[r, 2 * hh], wbuf[r, 2 * hh + 1]], axis=1)
                else:
                    right = wbuf[r, 2 * hh + half_of]
                part = jnp.dot(abuf[2 * hh + token_low, cc], right, preferred_element_type=F32)
                acc = part if acc is None else acc + part
            rows = pl.ds(pl.multiple_of(cc * ROWS, ROWS), ROWS)
            if half_of is None:
                cstage[tl, r, 0, rows, :] = acc[:, :LANES].astype(BF16)
                cstage[tl, r, 1, rows, :] = acc[:, LANES:].astype(BF16)
            else:
                cstage[tl, r, half_of, rows, :] = acc.astype(BF16)

        for ll in (0, 1) if half_of is None else (half_of,):
            send_part(tl, r, ll)

    arrived(abuf.at[y, 1 - core], cf_r.at[0])
    arrived(abuf.at[down, 1 - core, half[0]], cf_r.at[1])
    arrived(abuf.at[up, 1 - core, half[1]], cf_r.at[2])
    arrived(abuf.at[down, 1 - core, half[1]], cf_r.at[3])
    arrived(abuf.at[up, 1 - core, half[0]], cf_r.at[4])
    task(1, 0)
    pass_on(3)
    task(1, 1)
    task(1, 3)
    arrived(abuf.at[far, core, half[0]], ar_r.at[0])
    to_core(far, half[0], 5)
    arrived(abuf.at[far, core, half[1]], ar_r.at[1])
    to_core(far, half[1], 6)
    arrived(abuf.at[far, 1 - core, half[0]], cf_r.at[5])
    arrived(abuf.at[far, 1 - core, half[1]], cf_r.at[6])
    for copy in k_loads:
        copy.wait()
    for dy in range(4):
        for dc in range(2):
            if dy or dc:
                push(kp.at[dy, dc], kz.at[high, low, core], k_s.at[dy, dc], k_r.at[dy, dc], near(0, dy, 0, dc))

    for g, to in ((1, other), (2, partner), (3, across)):
        push(se_part.at[g], se_pin.at[g], sp_s.at[g], sp_r.at[g], to)

    task(0, 0)
    task(0, 1)
    task(0, 3)

    for k in range(4):
        passed(k)
    task(1, 2)
    task(0, 2)

    for dy in range(4):
        for dc in range(2):
            if dy or dc:
                py = lax.rem(y + 4 - dy, 4)
                arrived(kz.at[lax.div(py, 2), lax.rem(py, 2), lax.rem(core + dc, 2)], k_r.at[dy, dc])

    own_x = lax.rem(z, 2) * 2
    first_e = jnp.where(lax.rem(own_x - x + 4, 4) == 2, 1, 0)
    for e in (first_e, 1 - first_e):
        for tl in (1, 0):
            token_low = low if tl == 0 else 1 - low
            total = cstage[tl, lax.rem(own_x + e - x + 4, 4), lax.div(z, 2)].astype(F32)
            for dz in (1, 2, 3):
                arrived(zbuf.at[dz, tl, e], zs_r.at[dz, tl, e])
                total = total + zbuf[dz, tl, e].astype(F32)
            total = total.astype(BF16).astype(F32)
            for cc in range(2):
                rows = slice(cc * ROWS, (cc + 1) * ROWS)
                value = kz[e, token_low, cc].astype(F32) * total[rows]
                red[e, token_low, pl.ds(cc * ROWS, ROWS), :] = value.astype(BF16)
            for pc in range(2):
                py = 2 * e + token_low
                dy, dc = lax.rem(py - y + 4, 4), lax.rem(pc - core + 2, 2)
                src = red.at[e, token_low, pl.ds(pc * ROWS, ROWS)]
                dst = xh.at[core * 4 + y, pl.ds(SPAN, ROWS)]
                copy = remote(src, dst, fs_s.at[dy, dc], fs_r.at[dy, dc], device(x, py, z, pc))
                here = dy + dc == 0
                z_sends.append((dy + dc, copy))

                @pl.when(dy + dc > 0)
                def _():
                    copy.start()

                @pl.when(here)
                def _():
                    xh[core * 4 + y, pl.ds(SPAN, ROWS), :] = red[e, token_low, pl.ds(pc * ROWS, ROWS), :]

        right = red[e].reshape(4 * ROWS, LANES)
        for r in (2, 1, 3, 0):
            left = pick[pl.ds(r * 4, 4)].reshape(4 * SPAN, 4 * ROWS)
            slot[e, r] = jnp.dot(left, right, preferred_element_type=F32).astype(BF16)
            if r:
                push(slot.at[e, r], slot_in.at[e, r], st_s.at[e, r], st_r.at[e, r], near(r, 0, 0, 0))

    for g in (1, 2, 3):
        arrived(se_pin.at[g], sp_r.at[g])
    se_sum = se_part[0].astype(F32) + se_pin[1].astype(F32) + se_pin[2].astype(F32) + se_pin[3].astype(F32)
    for r in range(4):
        rows = se_sum[8 * r : 8 * r + 8]
        se_slot[r] = jnp.concatenate([rows, jnp.zeros_like(rows)], axis=0).astype(BF16)
        if r:
            push(se_slot.at[r], se_sin.at[r], sq_s.at[r], sq_r.at[r], near(r, 0, 0, 0))

    for dy in range(4):
        for dc in range(2):
            if dy or dc:
                at = lax.rem(core + dc, 2) * 4 + lax.rem(y + 4 - dy, 4)
                arrived(xh.at[at, pl.ds(SPAN, ROWS)], fs_r.at[dy, dc])
    push(xh.at[:, pl.ds(ROWS, SPAN)], xh.at[:, pl.ds(0, SPAN)], mx_s.at[0], mx_r.at[0], after)
    gate_load.wait()

    def convolve(b):
        @pl.loop(0, WIDTH // LANES)
        def _(p):
            lanes = column(p)
            left = toep[b, pl.ds(p * 8, 8)].reshape(8 * SPAN, 2 * SPAN)
            big[...] = jnp.dot(left, xh[p, pl.ds(b * SPAN, 2 * SPAN), :], preferred_element_type=F32)
            group = lax.div(iota((SPAN, LANES), 1), 16)
            out = big[pl.ds(0, SPAN), :]
            for g in range(1, 8):
                out = jnp.where(group == g, big[pl.ds(g * SPAN, SPAN), :], out)
            rows = pl.ds(b * SPAN, SPAN)
            mixed[rows, lanes] = (gate[rows, lanes].astype(F32) * out).astype(BF16)

    convolve(1)

    def states(e):
        for r in (1, 2, 3):
            arrived(slot_in.at[e, r], st_r.at[e, r])
        slot_sum[e] = (
            slot[e, 0].astype(F32) + slot_in[e, 1].astype(F32) + slot_in[e, 2].astype(F32) + slot_in[e, 3].astype(F32)
        ).astype(BF16)
        for pl_, pc in ((0, 0), (0, 1), (1, 0), (1, 1)):
            py = 2 * e + pl_
            dy, dc = lax.rem(py - y + 4, 4), lax.rem(pc - core + 2, 2)
            rows = pl.ds((pl_ * 2 + pc) * SPAN, SPAN)
            copy = remote(
                slot_sum.at[e, rows], st.at[core * 4 + y], sy_s.at[dy, dc], sy_r.at[dy, dc], device(x, py, z, pc)
            )
            z_sends.append((dy + dc, copy))

            @pl.when(dy + dc > 0)
            def _():
                copy.start()

            @pl.when(dy + dc == 0)
            def _():
                st[core * 4 + y] = slot_sum[e, rows, :]

    arrived(xh.at[:, pl.ds(0, SPAN)], mx_r.at[0])
    convolve(0)
    states(first_e)
    states(1 - first_e)

    se_total = se_slot[0].astype(F32)
    for r in (1, 2, 3):
        arrived(se_sin.at[r], sq_r.at[r])
        se_total = se_total + se_sin[r].astype(F32)
    se_state[0] = se_total.astype(BF16)
    for dy in range(4):
        for dc in range(2):
            if dy or dc:
                at = lax.rem(core + dc, 2) * 4 + lax.rem(y + 4 - dy, 4)
                arrived(st.at[at], sy_r.at[dy, dc])
    for p in range(8):
        mr_state[0, :, pl.ds(p * LANES, LANES)] = st[p]

    for copy in sent:
        copy.wait_send()
    for away, copy in z_sends:

        @pl.when(away > 0)
        def _():
            copy.wait_send()


def finish(mixed_in, se_in, mr_in, mixed, se_state, mr_state):
    mixed[...] = mixed_in[...]
    se_state[...] = se_in[:, pl.ds(0, TAPS - 1), :]
    mr_state[...] = mr_in[:, pl.ds(0, SPAN - 1), :]


def on_device(feats_se, filt_se, w_out, feats_mr, filt_mr, lengths, owners):
    vmem, anywhere = pl.BlockSpec(memory_space=pltpu.VMEM), pl.BlockSpec(memory_space=pl.ANY)
    dma = pltpu.SemaphoreType.DMA
    scratch = [
        pltpu.SMEM((8,), I32), pltpu.SMEM((8,), I32),
        pltpu.VMEM((TAPS, 64), F32), pltpu.VMEM((64, SPAN), F32),
        pltpu.VMEM((3, ROWS, WIDTH), BF16),
        pltpu.VMEM((2, 16, WIDTH), BF16),
        pltpu.VMEM((ROWS, WIDTH), BF16),
        pltpu.VMEM((4, 2, ROWS, LANES), BF16),
        pltpu.VMEM((2, 2, 2, ROWS, LANES), BF16),
        pltpu.VMEM((ROWS + 16, WIDTH), F32),
        pltpu.VMEM((ROWS, LANES), I32),
        pltpu.VMEM((3, WIDTH, LANES), BF16),
        pltpu.VMEM((4, 4, WIDTH, LANES), BF16),
        pltpu.VMEM((4, 2, ROWS, WIDTH), BF16),
        pltpu.VMEM((2, 4, 2, 2 * ROWS, LANES), BF16),
        pltpu.VMEM((4, 2, 2, 2 * ROWS, LANES), BF16),
        pltpu.VMEM((2, 2, 2 * ROWS, LANES), BF16),
        pltpu.VMEM((64, SPAN), F32),
        pltpu.VMEM((2, 64, SPAN, 2 * SPAN), BF16),
        pltpu.VMEM((16, SPAN, 4 * ROWS), BF16),
        pltpu.VMEM((8, ROWS + SPAN, LANES), BF16),
        pltpu.VMEM((2, 4, 4 * SPAN, LANES), BF16),
        pltpu.VMEM((2, 4, 4 * SPAN, LANES), BF16),
        pltpu.VMEM((2, 4 * SPAN, LANES), BF16),
        pltpu.VMEM((8, SPAN, LANES), BF16),
        pltpu.VMEM((ROWS, WIDTH), BF16),
        pltpu.VMEM((4, 32, WIDTH), BF16),
        pltpu.VMEM((4, 32, WIDTH), BF16),
        pltpu.VMEM((4, 16, WIDTH), BF16),
        pltpu.VMEM((4, 16, WIDTH), BF16),
        pltpu.VMEM((8 * SPAN, LANES), F32),
        pltpu.VMEM((8, WIDTH), F32),
        dma((19,)), dma((2,)),
        dma((3,)), dma((3,)), dma((2, 4)), dma((2, 4)), dma((2, 4)), dma((2, 4)),
        dma((2, 2)), dma((2, 2)), dma((2,)), dma((2,)), dma((7,)), dma((7,)),
        dma((4, 2)), dma((4, 2)), dma((2, 4, 2)), dma((4, 2, 2)), dma((4, 2)), dma((4, 2)),
        dma((1,)), dma((1,)), dma((2, 4)), dma((2, 4)), dma((4, 2)), dma((4, 2)),
        dma((4,)), dma((4,)), dma((4,)), dma((4,)),
    ]
    results = pl.pallas_call(
        kernel,
        out_shape=(
            jax.ShapeDtypeStruct((ROWS, WIDTH), BF16),
            jax.ShapeDtypeStruct((1, 16, WIDTH), BF16),
            jax.ShapeDtypeStruct((1, SPAN, WIDTH), BF16),
        ),
        in_specs=[anywhere] * 7,
        out_specs=(vmem, vmem, vmem),
        scratch_shapes=scratch,
        compiler_params=pltpu.CompilerParams(
            collective_id=0, has_side_effects=True, vmem_limit_bytes=56 * 2**20
        ),
        cost_estimate=pl.CostEstimate(flops=5 * 10**9, bytes_accessed=5 * 10**6, transcendentals=0),
        name="hyena",
    )(lengths, owners, filt_se.T, filt_mr, feats_se, w_out, feats_mr)
    return pl.pallas_call(
        finish,
        out_shape=(
            jax.ShapeDtypeStruct((ROWS, WIDTH), BF16),
            jax.ShapeDtypeStruct((1, TAPS - 1, WIDTH), BF16),
            jax.ShapeDtypeStruct((1, SPAN - 1, WIDTH), BF16),
        ),
        in_specs=[vmem] * 3,
        out_specs=(vmem, vmem, vmem),
        compiler_params=pltpu.CompilerParams(vmem_limit_bytes=56 * 2**20),
        name="outputs",
    )(*results)


def solution(mesh):
    in_specs = (
        P(None, "ctx", "chan"),
        P("chan", None),
        P("chan", "ctx"),
        P(None, "ctx", "chan"),
        P("chan", None),
        P(),
        P(),
    )
    out_specs = (P("ctx", "chan"), P("ctx", None, "chan"), P("ctx", None, "chan"))
    return jax.shard_map(
        on_device, mesh=mesh, in_specs=in_specs, out_specs=out_specs, check_vma=False
    )
```

```python
import jax
import jax.numpy as jnp
from jax import lax
from jax.experimental import pallas as pl
from jax.experimental.pallas import tpu as pltpu
from jax.sharding import PartitionSpec as P

BF16, F32, I32 = jnp.bfloat16, jnp.float32, jnp.int32
MESH = pl.DeviceIdType.MESH
ROWS, WIDTH, LANES = 256, 1024, 128
TAPS, SPAN = 7, 128
FAR = 1 << 20


def iota(shape, axis):
    return lax.broadcasted_iota(I32, shape, axis)


def kernel(
    lengths_in, owners_in, filt_se_in, filt_mr_in, feats_se, w_out, feats_mr,
    mixed, se_state, mr_state,
    lengths, owners, filt_se, filt_mr,
    feat, halo, gate, kp, kz, se_in, rel, wq, wbuf, abuf, cstage, zh, zbuf, red, g0, toep, pick,
    xh, slot_half, slot, slot_in, slot_sum, st, se_bf, se_part, se_pin, se_slot, se_sin, big, taps,
    load_sem, halo_sem, ws_s, ws_r, xs_s, xs_r, rl_s, rl_r, as_s, as_r, ar_s, ar_r, cf_s, cf_r,
    k_s, k_r, zh_s, zh_r, zs_s, zs_r, fs_s, fs_r, hs_s, hs_r, st_s, st_r, sy_s, sy_r, sp_s, sp_r, sq_s, sq_r,
):
    ctx, chan = lax.axis_index("ctx"), lax.axis_index("chan")
    core, x, low = lax.rem(ctx, 2), lax.rem(lax.div(ctx, 2), 4), lax.div(ctx, 8)
    high, z = lax.rem(chan, 2), lax.div(chan, 2)
    y = high * 2 + low

    def device(px, py, pz, pc):
        return {"ctx": lax.rem(py, 2) * 8 + px * 2 + pc, "chan": pz * 2 + lax.div(py, 2)}

    def near(dx, dy, dz, dc):
        return device(lax.rem(x + dx, 4), lax.rem(y + dy, 4), lax.rem(z + dz, 4), lax.rem(core + dc, 2))

    other = near(0, 0, 0, 1)
    partner = device(x, high * 2 + 1 - low, z, core)
    across = device(x, high * 2 + 1 - low, z, 1 - core)
    after, before = {"ctx": lax.rem(ctx + 1, 16)}, {"ctx": lax.rem(ctx + 15, 16)}

    def remote(src, dst, send, recv, to):
        return pltpu.make_async_remote_copy(
            src_ref=src, dst_ref=dst, send_sem=send, recv_sem=recv, device_id=to, device_id_type=MESH
        )

    sent = []

    def push(src, dst, send, recv, to):
        copy = remote(src, dst, send, recv, to)
        copy.start()
        sent.append(copy)

    def arrived(ref, recv):
        remote(ref, ref, recv, recv, other).wait_recv()

    def load(src, dst, at):
        copy = pltpu.make_async_copy(src, dst, load_sem.at[at])
        copy.start()
        return copy

    def column(q):
        return pl.ds(pl.multiple_of(q * LANES, LANES), LANES)

    w_loads = [None] * 4
    for dy in (1, 3, 2, 0):
        src = w_out.at[:, column(lax.rem(y + dy, 4))]
        w_loads[dy] = load(src, wbuf.at[0, y] if dy == 0 else wq.at[dy - 1], dy)
    kv_load = load(feats_se.at[pl.ds(1, 2)], feat.at[pl.ds(1, 2)], 4)
    small = [load(lengths_in, lengths, 7), load(filt_se_in, filt_se, 9)]
    q_load = load(feats_se.at[0], feat.at[0], 5)
    late = [load(owners_in, owners, 8), load(filt_mr_in, filt_mr, 10)]
    gate_load = load(feats_mr.at[0], gate, 6)
    k_loads = []
    for dy in range(4):
        for dc in range(2):
            p = lax.rem(core + dc, 2) * 4 + lax.rem(y + dy, 4)
            dst = kp.at[dy, dc] if dy or dc else kz.at[high, low, core]
            k_loads.append(load(feats_mr.at[1, :, column(p)], dst, 11 + dy * 2 + dc))

    barrier = pltpu.get_barrier_semaphore()
    peers = [after, before]
    peers += [near(0, dy, 0, dc) for dy in range(4) for dc in range(2) if dy or dc]
    peers += [near(d, 0, 0, 0) for d in (1, 2, 3)] + [near(0, 0, d, 0) for d in (1, 2, 3)]
    for peer in peers:
        pl.semaphore_signal(barrier, inc=1, device_id=peer, device_id_type=MESH)

    @pl.when(core == 0)
    def _():
        for dy in range(4):
            for dc in range(2):
                pl.semaphore_signal(barrier, inc=1, device_id=near(3, dy, 0, dc), device_id_type=MESH)

    pl.semaphore_wait(barrier, len(peers) + 4)

    push(feats_se.at[pl.ds(1, 2), pl.ds(ROWS - 16, 16)], halo, halo_sem.at[0], halo_sem.at[1], after)
    for dy in (1, 3, 2):
        w_loads[dy].wait()
        push(wq.at[dy - 1], wbuf.at[0, y], ws_s.at[dy - 1], ws_r.at[dy - 1], near(0, dy, 0, 0))
    w_loads[0].wait()

    order = [y, lax.rem(y + 3, 4), lax.rem(y + 1, 4), lax.rem(y + 2, 4)]
    down, up, far = order[1], order[2], order[3]

    def spread(k):
        if k:
            arrived(wbuf.at[0, order[k]], ws_r.at[(0, 1, 3, 2)[k] - 1])
        push(wbuf.at[0, order[k]], wbuf.at[3, order[k]], xs_s.at[0, k], xs_r.at[0, k], near(1, 0, 0, 0))
        push(wbuf.at[0, order[k]], wbuf.at[1, order[k]], xs_s.at[1, k], xs_r.at[1, k], near(3, 0, 0, 0))

    def pass_on(k):
        half = WIDTH // 2
        first, second = pl.ds(0, half), pl.ds(half, half)
        arrived(wbuf.at[3, order[k]], xs_r.at[0, k])
        push(wbuf.at[3, order[k], first], wbuf.at[2, order[k], first], rl_s.at[0, k], rl_r.at[0, k], near(1, 0, 0, 0))
        arrived(wbuf.at[1, order[k]], xs_r.at[1, k])
        push(wbuf.at[1, order[k], second], wbuf.at[2, order[k], second], rl_s.at[1, k], rl_r.at[1, k], near(3, 0, 0, 0))

    def passed(k):
        half = WIDTH // 2
        arrived(wbuf.at[2, order[k], pl.ds(0, half)], rl_r.at[0, k])
        arrived(wbuf.at[2, order[k], pl.ds(half, half)], rl_r.at[1, k])

    spread(0)

    for copy in small:
        copy.wait()
    starts, ends = [], []
    total = jnp.int32(0)
    for r in range(8):
        starts.append(total)
        total = total + lengths[r]
        ends.append(total)
    pos = iota((ROWS, LANES), 0) + ctx * ROWS
    seg = jnp.zeros((ROWS, LANES), I32)
    for r in range(8):
        seg = jnp.maximum(seg, jnp.where(starts[r] <= pos, starts[r], 0))
    rel[...] = pos - seg

    spread_out = jnp.where(lax.div(iota((64, WIDTH), 1), 16) == iota((64, WIDTH), 0), 1.0, 0.0).astype(F32)
    taps[pl.ds(0, TAPS), :] = lax.dot_general(
        filt_se[...], spread_out, (((1,), (0,)), ((), ())),
        precision=lax.Precision.HIGHEST, preferred_element_type=F32,
    )
    kv_load.wait()
    se_in[pl.ds(16, ROWS), :] = feat[1].astype(F32) * feat[2].astype(F32)
    se_bf[...] = se_in[pl.ds(16, ROWS), :].astype(BF16)
    q_load.wait()

    def short(first, count):
        @pl.loop(0, WIDTH // LANES)
        def _(p):
            lanes = column(p)
            acc = jnp.zeros((count, LANES), F32)
            for j in range(TAPS):
                term = taps[pl.ds(j, 1), lanes] * se_in[pl.ds(16 + first - j, count), lanes]
                acc = acc + jnp.where(rel[pl.ds(first, count), :] >= j, term, 0.0)
            rows = pl.ds(first, count)
            abuf[y, core, rows, lanes] = (feat[0, rows, lanes].astype(F32) * acc).astype(BF16)

    short(16, ROWS - 16)
    arrived(halo, halo_sem.at[1])
    se_in[pl.ds(0, 16), :] = halo[0].astype(F32) * halo[1].astype(F32)
    short(0, 16)

    half = pl.ds(0, ROWS // 2), pl.ds(ROWS // 2, ROWS // 2)
    for i in range(2):
        for way in range(2):
            mine = abuf.at[y, core, half[i ^ way]]
            push(mine, mine, as_s.at[way, i], as_r.at[way, i], near(0, (1, 3)[way], 0, 0))
    mine = abuf.at[y, core]
    push(mine, mine, cf_s.at[0], cf_r.at[0], other)

    for copy in late:
        copy.wait()

    def request_at(target):
        end = jnp.int32(-FAR)
        start = jnp.int32(0)
        for r in range(8):
            end = jnp.where(owners[r] == target, ends[r], end)
            start = jnp.where(owners[r] == target, starts[r], start)
        return end, start

    def picker(end, start, base, span, rows):
        at = iota((rows, ROWS), 1) + base
        row = iota((rows, ROWS), 0)
        keep = (at == end - span + row) & (at >= start) & (row < span)
        return jnp.where(keep, 1.0, 0.0).astype(BF16)

    groups = [(low, core), (low, 1 - core), (1 - low, core), (1 - low, 1 - core)]
    for g, (to_low, to_core) in enumerate(groups):
        rows = []
        for r in range(4):
            end, start = request_at(to_low * 8 + lax.rem(x + r, 4) * 2 + to_core)
            rows.append(picker(end, start, ctx * ROWS, TAPS - 1, 8))
        se_part[g] = jnp.dot(
            jnp.concatenate(rows, axis=0), se_bf[...], preferred_element_type=F32
        ).astype(BF16)

    spread(1)
    spread(2)

    turn = jnp.where(lax.rem(iota((SPAN, SPAN), 0) + iota((SPAN, SPAN), 1), SPAN) == 0, 1.0, 0.0)
    g0[...] = jnp.dot(filt_mr[...].astype(BF16), turn.astype(BF16), preferred_element_type=F32)

    def band(first, count):
        @pl.loop(first, first + count)
        def _(g):
            ring = pltpu.roll(
                jnp.broadcast_to(g0[pl.ds(g, 1), :], (SPAN, SPAN)), 0, 1, stride=1, stride_axis=0
            )
            step = iota((SPAN, SPAN), 0) - iota((SPAN, SPAN), 1)
            for b in range(2):
                reach = rel[pl.ds(b * SPAN, SPAN), :]
                left = jnp.where((step < 0) & (step + SPAN <= reach), ring, 0.0)
                right = jnp.where((step >= 0) & (step <= reach), ring, 0.0)
                toep[b, g, :, pl.ds(0, SPAN)] = left.astype(BF16)
                toep[b, g, :, pl.ds(SPAN, SPAN)] = right.astype(BF16)

    band(0, 24)
    pass_on(0)
    spread(3)
    band(24, 40)

    @pl.loop(0, 16)
    def _(i):
        target = lax.rem(lax.div(i, 2), 2) * 8 + lax.rem(x + lax.div(i, 4), 4) * 2 + lax.rem(i, 2)
        end, start = request_at(target)
        for b in range(4):
            base = ((b // 2) * 8 + x * 2 + b % 2) * ROWS
            pick[i, :, pl.ds(b * ROWS, ROWS)] = picker(end, start, base, SPAN - 1, SPAN)

    pass_on(1)
    pass_on(2)
    def to_core(block, part, at):
        push(abuf.at[block, core, part], abuf.at[block, core, part], cf_s.at[at], cf_r.at[at], other)

    arrived(abuf.at[down, core, half[0]], as_r.at[0, 0])
    push(abuf.at[down, core, half[0]], abuf.at[down, core, half[0]], ar_s.at[0], ar_r.at[0], near(0, 1, 0, 0))
    to_core(down, half[0], 1)
    arrived(abuf.at[up, core, half[1]], as_r.at[1, 0])
    push(abuf.at[up, core, half[1]], abuf.at[up, core, half[1]], ar_s.at[1], ar_r.at[1], near(0, 3, 0, 0))
    to_core(up, half[1], 2)
    arrived(abuf.at[down, core, half[1]], as_r.at[0, 1])
    to_core(down, half[1], 3)
    arrived(abuf.at[up, core, half[0]], as_r.at[1, 1])
    to_core(up, half[0], 4)

    z_sends = []

    def when_push(cond, src, dst, send, recv, to):
        copy = remote(src, dst, send, recv, to)
        z_sends.append((cond, copy))

        @pl.when(cond)
        def _():
            copy.start()

    lo, hi = pl.ds(0, ROWS), pl.ds(ROWS, ROWS)
    above, below = near(0, 0, 1, 0), near(0, 0, 3, 0)
    to_above, to_below = lax.div(lax.rem(z + 1, 4), 2), lax.div(lax.rem(z + 3, 4), 2)

    def same_side(r):
        return lax.div(lax.rem(x + r, 4), 2) == lax.rem(z, 2)

    def task(tl, r):
        token_low = low if tl == 0 else 1 - low

        @pl.loop(0, 2)
        def _(cc):
            acc = None
            for hh in range(2):
                right = jnp.concatenate([wbuf[r, 2 * hh], wbuf[r, 2 * hh + 1]], axis=1)
                part = jnp.dot(abuf[2 * hh + token_low, cc], right, preferred_element_type=F32)
                acc = part if acc is None else acc + part
            rows = pl.ds(pl.multiple_of(cc * ROWS, ROWS), ROWS)
            cstage[tl, r, 0, rows, :] = acc[:, :LANES].astype(BF16)
            cstage[tl, r, 1, rows, :] = acc[:, LANES:].astype(BF16)

        opposite = cstage.at[tl, r, 1 - lax.div(z, 2)]
        same = same_side(r)
        when_push(same, opposite.at[lo], zh.at[tl, r, 0], zh_s.at[tl, r, 0], zh_r.at[tl, r, 0], above)
        when_push(same, opposite.at[hi], zh.at[tl, r, 1], zh_s.at[tl, r, 1], zh_r.at[tl, r, 1], below)

    def add_on(tl, r):
        other_side = jnp.logical_not(same_side(r))
        e = lax.rem(lax.rem(x + r, 4), 2)

        @pl.when(other_side)
        def _():
            arrived(zh.at[tl, r, 0], zh_r.at[tl, r, 0])
            mine = cstage[tl, r, to_above, lo, :].astype(F32)
            cstage[tl, r, to_above, lo, :] = (mine + zh[tl, r, 0].astype(F32)).astype(BF16)

        when_push(
            other_side, cstage.at[tl, r, to_above], zbuf.at[0, tl, e], zs_s.at[tl, r, 0], zs_r.at[0, tl, e], above
        )

        @pl.when(other_side)
        def _():
            arrived(zh.at[tl, r, 1], zh_r.at[tl, r, 1])
            mine = cstage[tl, r, to_below, hi, :].astype(F32)
            cstage[tl, r, to_below, hi, :] = (mine + zh[tl, r, 1].astype(F32)).astype(BF16)

        when_push(
            other_side, cstage.at[tl, r, to_below], zbuf.at[1, tl, e], zs_s.at[tl, r, 1], zs_r.at[1, tl, e], below
        )

    arrived(abuf.at[y, 1 - core], cf_r.at[0])
    arrived(abuf.at[down, 1 - core, half[0]], cf_r.at[1])
    arrived(abuf.at[up, 1 - core, half[1]], cf_r.at[2])
    arrived(abuf.at[down, 1 - core, half[1]], cf_r.at[3])
    arrived(abuf.at[up, 1 - core, half[0]], cf_r.at[4])
    task(1, 0)
    pass_on(3)
    task(1, 1)
    task(1, 3)
    add_on(1, 0)
    arrived(abuf.at[far, core, half[0]], ar_r.at[0])
    to_core(far, half[0], 5)
    arrived(abuf.at[far, core, half[1]], ar_r.at[1])
    to_core(far, half[1], 6)
    arrived(abuf.at[far, 1 - core, half[0]], cf_r.at[5])
    arrived(abuf.at[far, 1 - core, half[1]], cf_r.at[6])
    for copy in k_loads:
        copy.wait()
    for dy in range(4):
        for dc in range(2):
            if dy or dc:
                push(kp.at[dy, dc], kz.at[high, low, core], k_s.at[dy, dc], k_r.at[dy, dc], near(0, dy, 0, dc))

    for g, to in ((1, other), (2, partner), (3, across)):
        push(se_part.at[g], se_pin.at[g], sp_s.at[g], sp_r.at[g], to)

    add_on(1, 1)
    add_on(1, 3)
    task(0, 0)
    task(0, 1)
    task(0, 3)

    for k in range(4):
        passed(k)
    task(1, 2)
    task(0, 2)
    for add_tl, add_r in ((0, 0), (0, 1), (0, 3), (1, 2), (0, 2)):
        add_on(add_tl, add_r)

    for dy in range(4):
        for dc in range(2):
            if dy or dc:
                py = lax.rem(y + 4 - dy, 4)
                arrived(kz.at[lax.div(py, 2), lax.rem(py, 2), lax.rem(core + dc, 2)], k_r.at[dy, dc])

    own_x = lax.rem(z, 2) * 2
    first_e = jnp.where(lax.rem(own_x - x + 4, 4) == 2, 1, 0)
    for e in (first_e, 1 - first_e):
        for tl in (1, 0):
            token_low = low if tl == 0 else 1 - low
            total = cstage[tl, lax.rem(own_x + e - x + 4, 4), lax.div(z, 2)].astype(F32)
            for way in range(2):
                arrived(zbuf.at[way, tl, e], zs_r.at[way, tl, e])
                total = total + zbuf[way, tl, e].astype(F32)
            total = total.astype(BF16).astype(F32)
            for cc in range(2):
                rows = slice(cc * ROWS, (cc + 1) * ROWS)
                value = kz[e, token_low, cc].astype(F32) * total[rows]
                red[e, token_low, pl.ds(cc * ROWS, ROWS), :] = value.astype(BF16)
            for pc in range(2):
                py = 2 * e + token_low
                dy, dc = lax.rem(py - y + 4, 4), lax.rem(pc - core + 2, 2)
                src = red.at[e, token_low, pl.ds(pc * ROWS, ROWS)]
                dst = xh.at[core * 4 + y, pl.ds(SPAN, ROWS)]
                when_push(dy + dc > 0, src, dst, fs_s.at[dy, dc], fs_r.at[dy, dc], device(x, py, z, pc))

                @pl.when(dy + dc == 0)
                def _():
                    xh[core * 4 + y, pl.ds(SPAN, ROWS), :] = red[e, token_low, pl.ds(pc * ROWS, ROWS), :]

                last = red.at[e, token_low, pl.ds(pc * ROWS + SPAN, SPAN)]
                edge = xh.at[core * 4 + y, pl.ds(0, SPAN)]
                if pc == 0:
                    following = device(x, py, z, 1)
                    away = dy + (1 - core) > 0
                else:
                    wrap = lax.div(x, 3)
                    next_low = token_low + wrap - 2 * token_low * wrap
                    following = device(lax.rem(x + 1, 4), 2 * e + next_low, z, 0)
                    away = dy >= 0
                at = tl * 2 + pc
                when_push(away, last, edge, hs_s.at[e, at], hs_r.at[core * 4 + y], following)
                if pc == 0:

                    @pl.when(jnp.logical_not(away))
                    def _():
                        xh[core * 4 + y, pl.ds(0, SPAN), :] = red[e, token_low, pl.ds(SPAN, SPAN), :]

            right = red[e, token_low]
            lanes = pl.ds(pl.multiple_of(token_low * 2 * ROWS, 2 * ROWS), 2 * ROWS)
            for r in (2, 1, 3, 0):
                left = pick[pl.ds(r * 4, 4), :, lanes].reshape(4 * SPAN, 2 * ROWS)
                some = jnp.dot(left, right, preferred_element_type=F32)
                if tl == 1:
                    slot_half[r] = some
                    continue
                slot[e, r] = (slot_half[r] + some).astype(BF16)
                if r:
                    push(slot.at[e, r], slot_in.at[e, r], st_s.at[e, r], st_r.at[e, r], near(r, 0, 0, 0))

    for g in (1, 2, 3):
        arrived(se_pin.at[g], sp_r.at[g])
    se_sum = se_part[0].astype(F32) + se_pin[1].astype(F32) + se_pin[2].astype(F32) + se_pin[3].astype(F32)
    for r in range(4):
        rows = se_sum[8 * r : 8 * r + 8]
        se_slot[r] = jnp.concatenate([rows, jnp.zeros_like(rows)], axis=0).astype(BF16)
        if r:
            push(se_slot.at[r], se_sin.at[r], sq_s.at[r], sq_r.at[r], near(r, 0, 0, 0))

    for dy in range(4):
        for dc in range(2):
            if dy or dc:
                at = lax.rem(core + dc, 2) * 4 + lax.rem(y + 4 - dy, 4)
                arrived(xh.at[at, pl.ds(SPAN, ROWS)], fs_r.at[dy, dc])
    gate_load.wait()

    def convolve(b):
        @pl.loop(0, WIDTH // LANES)
        def _(p):
            lanes = column(p)
            left = toep[b, pl.ds(p * 8, 8)].reshape(8 * SPAN, 2 * SPAN)
            big[...] = jnp.dot(left, xh[p, pl.ds(b * SPAN, 2 * SPAN), :], preferred_element_type=F32)
            group = lax.div(iota((SPAN, LANES), 1), 16)
            out = big[pl.ds(0, SPAN), :]
            for g in range(1, 8):
                out = jnp.where(group == g, big[pl.ds(g * SPAN, SPAN), :], out)
            rows = pl.ds(b * SPAN, SPAN)
            mixed[rows, lanes] = (gate[rows, lanes].astype(F32) * out).astype(BF16)

    convolve(1)

    def states(e):
        for r in (1, 2, 3):
            arrived(slot_in.at[e, r], st_r.at[e, r])
        slot_sum[e] = (
            slot[e, 0].astype(F32) + slot_in[e, 1].astype(F32) + slot_in[e, 2].astype(F32) + slot_in[e, 3].astype(F32)
        ).astype(BF16)
        for pl_, pc in ((0, 0), (0, 1), (1, 0), (1, 1)):
            py = 2 * e + pl_
            dy, dc = lax.rem(py - y + 4, 4), lax.rem(pc - core + 2, 2)
            rows = pl.ds((pl_ * 2 + pc) * SPAN, SPAN)
            when_push(
                dy + dc > 0, slot_sum.at[e, rows], st.at[core * 4 + y], sy_s.at[dy, dc], sy_r.at[dy, dc],
                device(x, py, z, pc),
            )

            @pl.when(dy + dc == 0)
            def _():
                st[core * 4 + y] = slot_sum[e, rows, :]

    for p in range(8):

        @pl.when((core == 0) | (p != core * 4 + y))
        def _():
            arrived(xh.at[p, pl.ds(0, SPAN)], hs_r.at[p])

    states(first_e)
    states(1 - first_e)
    convolve(0)

    se_total = se_slot[0].astype(F32)
    for r in (1, 2, 3):
        arrived(se_sin.at[r], sq_r.at[r])
        se_total = se_total + se_sin[r].astype(F32)
    se_state[0] = se_total.astype(BF16)
    for dy in range(4):
        for dc in range(2):
            if dy or dc:
                at = lax.rem(core + dc, 2) * 4 + lax.rem(y + 4 - dy, 4)
                arrived(st.at[at], sy_r.at[dy, dc])
    for p in range(8):
        mr_state[0, :, pl.ds(p * LANES, LANES)] = st[p]

    for copy in sent:
        copy.wait_send()
    for cond, copy in z_sends:

        @pl.when(cond)
        def _():
            copy.wait_send()


def finish(mixed_in, se_in, mr_in, mixed, se_state, mr_state):
    mixed[...] = mixed_in[...]
    se_state[...] = se_in[:, pl.ds(0, TAPS - 1), :]
    mr_state[...] = mr_in[:, pl.ds(0, SPAN - 1), :]


def on_device(feats_se, filt_se, w_out, feats_mr, filt_mr, lengths, owners):
    vmem, anywhere = pl.BlockSpec(memory_space=pltpu.VMEM), pl.BlockSpec(memory_space=pl.ANY)
    dma = pltpu.SemaphoreType.DMA
    scratch = [
        pltpu.SMEM((8,), I32), pltpu.SMEM((8,), I32),
        pltpu.VMEM((TAPS, 64), F32), pltpu.VMEM((64, SPAN), F32),
        pltpu.VMEM((3, ROWS, WIDTH), BF16),
        pltpu.VMEM((2, 16, WIDTH), BF16),
        pltpu.VMEM((ROWS, WIDTH), BF16),
        pltpu.VMEM((4, 2, ROWS, LANES), BF16),
        pltpu.VMEM((2, 2, 2, ROWS, LANES), BF16),
        pltpu.VMEM((ROWS + 16, WIDTH), F32),
        pltpu.VMEM((ROWS, LANES), I32),
        pltpu.VMEM((3, WIDTH, LANES), BF16),
        pltpu.VMEM((4, 4, WIDTH, LANES), BF16),
        pltpu.VMEM((4, 2, ROWS, WIDTH), BF16),
        pltpu.VMEM((2, 4, 2, 2 * ROWS, LANES), BF16),
        pltpu.VMEM((2, 4, 2, ROWS, LANES), BF16),
        pltpu.VMEM((2, 2, 2, 2 * ROWS, LANES), BF16),
        pltpu.VMEM((2, 2, 2 * ROWS, LANES), BF16),
        pltpu.VMEM((64, SPAN), F32),
        pltpu.VMEM((2, 64, SPAN, 2 * SPAN), BF16),
        pltpu.VMEM((16, SPAN, 4 * ROWS), BF16),
        pltpu.VMEM((8, ROWS + SPAN, LANES), BF16),
        pltpu.VMEM((4, 4 * SPAN, LANES), F32),
        pltpu.VMEM((2, 4, 4 * SPAN, LANES), BF16),
        pltpu.VMEM((2, 4, 4 * SPAN, LANES), BF16),
        pltpu.VMEM((2, 4 * SPAN, LANES), BF16),
        pltpu.VMEM((8, SPAN, LANES), BF16),
        pltpu.VMEM((ROWS, WIDTH), BF16),
        pltpu.VMEM((4, 32, WIDTH), BF16),
        pltpu.VMEM((4, 32, WIDTH), BF16),
        pltpu.VMEM((4, 16, WIDTH), BF16),
        pltpu.VMEM((4, 16, WIDTH), BF16),
        pltpu.VMEM((8 * SPAN, LANES), F32),
        pltpu.VMEM((8, WIDTH), F32),
        dma((19,)), dma((2,)),
        dma((3,)), dma((3,)), dma((2, 4)), dma((2, 4)), dma((2, 4)), dma((2, 4)),
        dma((2, 2)), dma((2, 2)), dma((2,)), dma((2,)), dma((7,)), dma((7,)),
        dma((4, 2)), dma((4, 2)), dma((2, 4, 2)), dma((2, 4, 2)), dma((2, 4, 2)), dma((2, 2, 2)), dma((4, 2)), dma((4, 2)),
        dma((2, 4)), dma((8,)), dma((2, 4)), dma((2, 4)), dma((4, 2)), dma((4, 2)),
        dma((4,)), dma((4,)), dma((4,)), dma((4,)),
    ]
    results = pl.pallas_call(
        kernel,
        out_shape=(
            jax.ShapeDtypeStruct((ROWS, WIDTH), BF16),
            jax.ShapeDtypeStruct((1, 16, WIDTH), BF16),
            jax.ShapeDtypeStruct((1, SPAN, WIDTH), BF16),
        ),
        in_specs=[anywhere] * 7,
        out_specs=(vmem, vmem, vmem),
        scratch_shapes=scratch,
        compiler_params=pltpu.CompilerParams(
            collective_id=0, has_side_effects=True, vmem_limit_bytes=56 * 2**20
        ),
        cost_estimate=pl.CostEstimate(flops=5 * 10**9, bytes_accessed=5 * 10**6, transcendentals=0),
        name="hyena",
    )(lengths, owners, filt_se.T, filt_mr, feats_se, w_out, feats_mr)
    return pl.pallas_call(
        finish,
        out_shape=(
            jax.ShapeDtypeStruct((ROWS, WIDTH), BF16),
            jax.ShapeDtypeStruct((1, TAPS - 1, WIDTH), BF16),
            jax.ShapeDtypeStruct((1, SPAN - 1, WIDTH), BF16),
        ),
        in_specs=[vmem] * 3,
        out_specs=(vmem, vmem, vmem),
        compiler_params=pltpu.CompilerParams(vmem_limit_bytes=56 * 2**20),
        name="outputs",
    )(*results)


def solution(mesh):
    in_specs = (
        P(None, "ctx", "chan"),
        P("chan", None),
        P("chan", "ctx"),
        P(None, "ctx", "chan"),
        P("chan", None),
        P(),
        P(),
    )
    out_specs = (P("ctx", "chan"), P("ctx", None, "chan"), P("ctx", None, "chan"))
    return jax.shard_map(
        on_device, mesh=mesh, in_specs=in_specs, out_specs=out_specs, check_vma=False
    )
```

```python
import jax
import jax.numpy as jnp
from jax import lax
from jax.experimental import pallas as pl
from jax.experimental.pallas import tpu as pltpu
from jax.sharding import PartitionSpec as P

BF16, F32, I32 = jnp.bfloat16, jnp.float32, jnp.int32
MESH = pl.DeviceIdType.MESH
ROWS, WIDTH, LANES = 256, 1024, 128
TAPS, SPAN = 7, 128
FAR = 1 << 20


def iota(shape, axis):
    return lax.broadcasted_iota(I32, shape, axis)


def kernel(
    lengths_in, owners_in, filt_se_in, filt_mr_in, feats_se, w_out, feats_mr,
    mixed_out, se_out, mr_out,
    lengths, owners, filt_se, filt_mr, mixed, se_state, mr_state,
    feat, halo, gate, kp, kz, se_in, rel, wq, wbuf, abuf, cstage, zh, zbuf, red, g0, toep, pick,
    xh, slot_half, slot, slot_in, slot_sum, st, se_bf, se_part, se_pin, se_slot, se_sin, big, taps,
    load_sem, out_sem, halo_r, ws_r, xs_r, rl_r, as_r, ar_r, cf_r, k_r, zh_r, zs_r, fs_r, hs_r, st_r, sy_r, sp_r, sq_r,
):
    ctx, chan = lax.axis_index("ctx"), lax.axis_index("chan")
    core, x, low = lax.rem(ctx, 2), lax.rem(lax.div(ctx, 2), 4), lax.div(ctx, 8)
    high, z = lax.rem(chan, 2), lax.div(chan, 2)
    y = high * 2 + low

    def device(px, py, pz, pc):
        return {"ctx": lax.rem(py, 2) * 8 + px * 2 + pc, "chan": pz * 2 + lax.div(py, 2)}

    def near(dx, dy, dz, dc):
        return device(lax.rem(x + dx, 4), lax.rem(y + dy, 4), lax.rem(z + dz, 4), lax.rem(core + dc, 2))

    other = near(0, 0, 0, 1)
    partner = device(x, high * 2 + 1 - low, z, core)
    across = device(x, high * 2 + 1 - low, z, 1 - core)
    after, before = {"ctx": lax.rem(ctx + 1, 16)}, {"ctx": lax.rem(ctx + 15, 16)}

    def remote(src, dst, send, recv, to):
        return pltpu.make_async_remote_copy(
            src_ref=src, dst_ref=dst, send_sem=send, recv_sem=recv, device_id=to, device_id_type=MESH
        )

    (
        halo_s, ws_s, xs_s, rl_s, as_s, ar_s, cf_s, k_s, zh_s, zs_s, fs_s, hs_s, st_s, sy_s, sp_s, sq_s,
    ) = [out_sem.at[i] for i in range(16)]

    def push(src, dst, send, recv, to):
        remote(src, dst, send, recv, to).start()

    def arrived(ref, recv):
        remote(ref, ref, recv, recv, other).wait_recv()

    def load(src, dst, at):
        copy = pltpu.make_async_copy(src, dst, load_sem.at[at])
        copy.start()
        return copy

    def column(q):
        return pl.ds(pl.multiple_of(q * LANES, LANES), LANES)

    barrier = pltpu.get_barrier_semaphore()
    peers = [after, before]
    peers += [near(0, dy, 0, dc) for dy in range(4) for dc in range(2) if dy or dc]
    peers += [near(d, 0, 0, 0) for d in (1, 2, 3)] + [near(0, 0, d, 0) for d in (1, 2, 3)]
    for peer in peers:
        pl.semaphore_signal(barrier, inc=1, device_id=peer, device_id_type=MESH)

    @pl.when(core == 0)
    def _():
        for dy in range(4):
            for dc in range(2):
                pl.semaphore_signal(barrier, inc=1, device_id=near(3, dy, 0, dc), device_id_type=MESH)

    w_loads = [None] * 4
    for dy in (1, 3, 2, 0):
        src = w_out.at[:, column(lax.rem(y + dy, 4))]
        w_loads[dy] = load(src, wbuf.at[0, y] if dy == 0 else wq.at[dy - 1], dy)
    kv_load = load(feats_se.at[pl.ds(1, 2)], feat.at[pl.ds(1, 2)], 4)
    small = [load(lengths_in, lengths, 7), load(filt_se_in, filt_se, 9)]
    q_load = load(feats_se.at[0], feat.at[0], 5)
    late = [load(owners_in, owners, 8), load(filt_mr_in, filt_mr, 10)]
    gate_load = load(feats_mr.at[0], gate, 6)
    k_loads = []
    for dy in range(4):
        for dc in range(2):
            p = lax.rem(core + dc, 2) * 4 + lax.rem(y + dy, 4)
            dst = kp.at[dy, dc] if dy or dc else kz.at[high, low, core]
            k_loads.append(load(feats_mr.at[1, :, column(p)], dst, 11))

    pl.semaphore_wait(barrier, len(peers) + 4)

    push(feats_se.at[pl.ds(1, 2), pl.ds(ROWS - 16, 16)], halo, halo_s, halo_r.at[0], after)
    for dy in (1, 3, 2):
        w_loads[dy].wait()
        push(wq.at[dy - 1], wbuf.at[0, y], ws_s, ws_r.at[dy - 1], near(0, dy, 0, 0))
    w_loads[0].wait()

    order = [y, lax.rem(y + 3, 4), lax.rem(y + 1, 4), lax.rem(y + 2, 4)]
    down, up, far = order[1], order[2], order[3]

    def spread(k):
        if k:
            arrived(wbuf.at[0, order[k]], ws_r.at[(0, 1, 3, 2)[k] - 1])
        push(wbuf.at[0, order[k]], wbuf.at[3, order[k]], xs_s, xs_r.at[0, k], near(1, 0, 0, 0))
        push(wbuf.at[0, order[k]], wbuf.at[1, order[k]], xs_s, xs_r.at[1, k], near(3, 0, 0, 0))

    def pass_on(k):
        half = WIDTH // 2
        first, second = pl.ds(0, half), pl.ds(half, half)
        arrived(wbuf.at[3, order[k]], xs_r.at[0, k])
        push(wbuf.at[3, order[k], first], wbuf.at[2, order[k], first], rl_s, rl_r.at[0], near(1, 0, 0, 0))
        arrived(wbuf.at[1, order[k]], xs_r.at[1, k])
        push(wbuf.at[1, order[k], second], wbuf.at[2, order[k], second], rl_s, rl_r.at[0], near(3, 0, 0, 0))

    spread(0)

    for copy in small:
        copy.wait()
    starts, ends = [], []
    total = jnp.int32(0)
    for r in range(8):
        starts.append(total)
        total = total + lengths[r]
        ends.append(total)
    pos = iota((ROWS, LANES), 0) + ctx * ROWS
    seg = jnp.zeros((ROWS, LANES), I32)
    for r in range(8):
        seg = jnp.maximum(seg, jnp.where(starts[r] <= pos, starts[r], 0))
    rel[...] = pos - seg

    spread_out = jnp.where(lax.div(iota((64, WIDTH), 1), 16) == iota((64, WIDTH), 0), 1.0, 0.0).astype(F32)
    taps[pl.ds(0, TAPS), :] = lax.dot_general(
        filt_se[...], spread_out, (((1,), (0,)), ((), ())),
        precision=lax.Precision.HIGHEST, preferred_element_type=F32,
    )
    kv_load.wait()
    se_in[pl.ds(16, ROWS), :] = feat[1].astype(F32) * feat[2].astype(F32)
    se_bf[...] = se_in[pl.ds(16, ROWS), :].astype(BF16)
    q_load.wait()

    def short(first, count):
        @pl.loop(0, WIDTH // LANES)
        def _(p):
            lanes = column(p)
            acc = jnp.zeros((count, LANES), F32)
            for j in range(TAPS):
                term = taps[pl.ds(j, 1), lanes] * se_in[pl.ds(16 + first - j, count), lanes]
                acc = acc + jnp.where(rel[pl.ds(first, count), :] >= j, term, 0.0)
            rows = pl.ds(first, count)
            abuf[y, core, rows, lanes] = (feat[0, rows, lanes].astype(F32) * acc).astype(BF16)

    short(16, ROWS - 16)
    arrived(halo, halo_r.at[0])
    se_in[pl.ds(0, 16), :] = halo[0].astype(F32) * halo[1].astype(F32)
    short(0, 16)

    half = pl.ds(0, ROWS // 2), pl.ds(ROWS // 2, ROWS // 2)
    for i in range(2):
        for way in range(2):
            mine = abuf.at[y, core, half[i ^ way]]
            push(mine, mine, as_s, as_r.at[way, i], near(0, (1, 3)[way], 0, 0))
    mine = abuf.at[y, core]
    push(mine, mine, cf_s, cf_r.at[0], other)

    for copy in late:
        copy.wait()

    def request_at(target):
        end = jnp.int32(-FAR)
        start = jnp.int32(0)
        for r in range(8):
            end = jnp.where(owners[r] == target, ends[r], end)
            start = jnp.where(owners[r] == target, starts[r], start)
        return end, start

    def picker(end, start, base, span, rows):
        at = iota((rows, ROWS), 1) + base
        row = iota((rows, ROWS), 0)
        keep = (at == end - span + row) & (at >= start) & (row < span)
        return jnp.where(keep, 1.0, 0.0).astype(BF16)

    groups = [(low, core), (low, 1 - core), (1 - low, core), (1 - low, 1 - core)]
    for g, (to_low, to_core) in enumerate(groups):
        rows = []
        for r in range(4):
            end, start = request_at(to_low * 8 + lax.rem(x + r, 4) * 2 + to_core)
            rows.append(picker(end, start, ctx * ROWS, TAPS - 1, 8))
        se_part[g] = jnp.dot(
            jnp.concatenate(rows, axis=0), se_bf[...], preferred_element_type=F32
        ).astype(BF16)

    spread(1)
    spread(2)

    turn = jnp.where(lax.rem(iota((SPAN, SPAN), 0) + iota((SPAN, SPAN), 1), SPAN) == 0, 1.0, 0.0)
    g0[...] = jnp.dot(filt_mr[...].astype(BF16), turn.astype(BF16), preferred_element_type=F32)

    def band(first, count):
        @pl.loop(first, first + count)
        def _(g):
            ring = pltpu.roll(
                jnp.broadcast_to(g0[pl.ds(g, 1), :], (SPAN, SPAN)), 0, 1, stride=1, stride_axis=0
            )
            step = iota((SPAN, SPAN), 0) - iota((SPAN, SPAN), 1)
            for b in range(2):
                reach = rel[pl.ds(b * SPAN, SPAN), :]
                left = jnp.where((step < 0) & (step + SPAN <= reach), ring, 0.0)
                right = jnp.where((step >= 0) & (step <= reach), ring, 0.0)
                toep[b, g, :, pl.ds(0, SPAN)] = left.astype(BF16)
                toep[b, g, :, pl.ds(SPAN, SPAN)] = right.astype(BF16)

    band(0, 24)
    pass_on(0)
    spread(3)
    band(24, 40)

    @pl.loop(0, 16)
    def _(i):
        target = lax.rem(lax.div(i, 2), 2) * 8 + lax.rem(x + lax.div(i, 4), 4) * 2 + lax.rem(i, 2)
        end, start = request_at(target)
        for b in range(4):
            base = ((b // 2) * 8 + x * 2 + b % 2) * ROWS
            pick[i, :, pl.ds(b * ROWS, ROWS)] = picker(end, start, base, SPAN - 1, SPAN)

    pass_on(1)
    pass_on(2)
    def to_core(block, part, at):
        push(abuf.at[block, core, part], abuf.at[block, core, part], cf_s, cf_r.at[at], other)

    arrived(abuf.at[down, core, half[0]], as_r.at[0, 0])
    push(abuf.at[down, core, half[0]], abuf.at[down, core, half[0]], ar_s, ar_r.at[0], near(0, 1, 0, 0))
    to_core(down, half[0], 0)
    arrived(abuf.at[up, core, half[1]], as_r.at[1, 0])
    push(abuf.at[up, core, half[1]], abuf.at[up, core, half[1]], ar_s, ar_r.at[1], near(0, 3, 0, 0))
    to_core(up, half[1], 0)
    arrived(abuf.at[down, core, half[1]], as_r.at[0, 1])
    to_core(down, half[1], 0)
    arrived(abuf.at[up, core, half[0]], as_r.at[1, 1])
    to_core(up, half[0], 0)

    def when_push(cond, src, dst, send, recv, to):
        @pl.when(cond)
        def _():
            push(src, dst, send, recv, to)

    lo, hi = pl.ds(0, ROWS), pl.ds(ROWS, ROWS)
    above, below = near(0, 0, 1, 0), near(0, 0, 3, 0)
    to_above, to_below = lax.div(lax.rem(z + 1, 4), 2), lax.div(lax.rem(z + 3, 4), 2)

    def same_side(r):
        return lax.div(lax.rem(x + r, 4), 2) == lax.rem(z, 2)

    def product(tl, r, blocks):
        acc = None
        for hh in range(2):
            right = jnp.concatenate([wbuf[r, 2 * hh], wbuf[r, 2 * hh + 1]], axis=1)
            part = jnp.dot(blocks(2 * hh + (low if tl == 0 else 1 - low)), right, preferred_element_type=F32)
            acc = part if acc is None else acc + part
        return acc

    def half_copy(tl, r, cc):
        rows = pl.ds(pl.multiple_of(cc * ROWS, ROWS), ROWS)
        return remote(
            cstage.at[tl, r, 1 - lax.div(z, 2), rows], zh.at[tl, r, cc], zh_s, zh_r.at[tl, r, cc],
            near(0, 0, 1 + 2 * cc, 0),
        )

    def tasks(tl, turns, ready=None):
        @pl.loop(0, 2)
        def _(i):
            cc = lax.rem(core + i, 2)

            if ready is not None:

                @pl.when(i == 1)
                def _():
                    ready()

            for r in turns:
                acc = product(tl, r, lambda block: abuf[block, cc])
                rows = pl.ds(pl.multiple_of(cc * ROWS, ROWS), ROWS)
                cstage[tl, r, 0, rows, :] = acc[:, :LANES].astype(BF16)
                cstage[tl, r, 1, rows, :] = acc[:, LANES:].astype(BF16)

                @pl.when(same_side(r))
                def _():
                    half_copy(tl, r, cc).start()

    def add_on(tl, r):
        other_side = jnp.logical_not(same_side(r))
        e = lax.rem(lax.rem(x + r, 4), 2)

        @pl.when(other_side)
        def _():
            arrived(zh.at[tl, r, 0], zh_r.at[tl, r, 0])
            mine = cstage[tl, r, to_above, lo, :].astype(F32)
            cstage[tl, r, to_above, lo, :] = (mine + zh[tl, r, 0].astype(F32)).astype(BF16)

        when_push(
            other_side, cstage.at[tl, r, to_above], zbuf.at[0, tl, e], zs_s, zs_r.at[0, tl, e], above
        )

        @pl.when(other_side)
        def _():
            arrived(zh.at[tl, r, 1], zh_r.at[tl, r, 1])
            mine = cstage[tl, r, to_below, hi, :].astype(F32)
            cstage[tl, r, to_below, hi, :] = (mine + zh[tl, r, 1].astype(F32)).astype(BF16)

        when_push(
            other_side, cstage.at[tl, r, to_below], zbuf.at[1, tl, e], zs_s, zs_r.at[1, tl, e], below
        )

    def near_ready():
        arrived(feat, cf_r.at[0])

    tasks(1, (0,), near_ready)
    pass_on(3)
    tasks(1, (1,))
    add_on(1, 0)
    tasks(1, (3,))
    arrived(abuf.at[far, core, half[0]], ar_r.at[0])
    to_core(far, half[0], 1)
    arrived(abuf.at[far, core, half[1]], ar_r.at[1])
    to_core(far, half[1], 1)
    pltpu.make_async_copy(kp, kp, load_sem.at[11]).wait()
    for dy in range(4):
        for dc in range(2):
            if dy or dc:
                push(kp.at[dy, dc], kz.at[high, low, core], k_s, k_r.at[0], near(0, dy, 0, dc))

    for g, to in ((1, other), (2, partner), (3, across)):
        push(se_part.at[g], se_pin.at[g], sp_s, sp_r.at[0], to)

    def far_ready():
        arrived(abuf.at[far, 1 - core], cf_r.at[1])

    tasks(0, (0,), far_ready)
    add_on(1, 1)
    tasks(0, (1,))
    add_on(1, 3)
    tasks(0, (3,))

    arrived(wbuf.at[2], rl_r.at[0])
    tasks(1, (2,))
    tasks(0, (2,))
    for add_tl, add_r in ((0, 0), (0, 1), (0, 3), (1, 2), (0, 2)):
        add_on(add_tl, add_r)

    arrived(abuf.at[0, 0, pl.ds(0, 224)], k_r.at[0])

    own_x = lax.rem(z, 2) * 2
    first_e = jnp.where(lax.rem(own_x - x + 4, 4) == 2, 1, 0)
    for e in (first_e, 1 - first_e):
        for tl in (1, 0):
            token_low = low if tl == 0 else 1 - low
            total = cstage[tl, lax.rem(own_x + e - x + 4, 4), lax.div(z, 2)].astype(F32)
            for way in range(2):
                arrived(zbuf.at[way, tl, e], zs_r.at[way, tl, e])
                total = total + zbuf[way, tl, e].astype(F32)
            total = total.astype(BF16).astype(F32)
            for cc in range(2):
                rows = slice(cc * ROWS, (cc + 1) * ROWS)
                value = kz[e, token_low, cc].astype(F32) * total[rows]
                red[e, token_low, pl.ds(cc * ROWS, ROWS), :] = value.astype(BF16)
            for pc in range(2):
                py = 2 * e + token_low
                dy, dc = lax.rem(py - y + 4, 4), lax.rem(pc - core + 2, 2)
                src = red.at[e, token_low, pl.ds(pc * ROWS, ROWS)]
                dst = xh.at[core * 4 + y, pl.ds(SPAN, ROWS)]
                when_push(dy + dc > 0, src, dst, fs_s, fs_r.at[0], device(x, py, z, pc))

                @pl.when(dy + dc == 0)
                def _():
                    xh[core * 4 + y, pl.ds(SPAN, ROWS), :] = red[e, token_low, pl.ds(pc * ROWS, ROWS), :]

            right = red[e, token_low]
            lanes = pl.ds(pl.multiple_of(token_low * 2 * ROWS, 2 * ROWS), 2 * ROWS)
            for r in (2, 1, 3, 0):
                left = pick[pl.ds(r * 4, 4), :, lanes].reshape(4 * SPAN, 2 * ROWS)
                some = jnp.dot(left, right, preferred_element_type=F32)
                if tl == 1:
                    slot_half[r] = some
                    continue
                slot[e, r] = (slot_half[r] + some).astype(BF16)
                if r:
                    push(slot.at[e, r], slot_in.at[e, r], st_s, st_r.at[e], near(r, 0, 0, 0))

    for e in range(2):
        for token_low in range(2):
            for pc in range(2):
                py = 2 * e + token_low
                last = red.at[e, token_low, pl.ds(pc * ROWS + SPAN, SPAN)]
                edge = xh.at[core * 4 + y, pl.ds(0, SPAN)]
                if pc == 0:
                    following = device(x, py, z, 1)
                    away = (py != y) | (core == 0)
                else:
                    wrap = lax.div(x, 3)
                    next_low = token_low + wrap - 2 * token_low * wrap
                    following = device(lax.rem(x + 1, 4), 2 * e + next_low, z, 0)
                    away = core >= 0
                at = token_low * 2 + pc
                when_push(away, last, edge, hs_s, hs_r.at[0], following)
                if pc == 0:

                    @pl.when(jnp.logical_not(away))
                    def _():
                        xh[core * 4 + y, pl.ds(0, SPAN), :] = red[e, token_low, pl.ds(SPAN, SPAN), :]

    arrived(se_pin.at[pl.ds(1, 3)], sp_r.at[0])
    se_sum = se_part[0].astype(F32) + se_pin[1].astype(F32) + se_pin[2].astype(F32) + se_pin[3].astype(F32)
    for r in range(4):
        rows = se_sum[8 * r : 8 * r + 8]
        se_slot[r] = jnp.concatenate([rows, jnp.zeros_like(rows)], axis=0).astype(BF16)
        if r:
            push(se_slot.at[r], se_sin.at[r], sq_s, sq_r.at[0], near(r, 0, 0, 0))

    arrived(abuf.at[0, 0, pl.ds(0, 224)], fs_r.at[0])
    gate_load.wait()

    def convolve(b):
        @pl.loop(0, WIDTH // LANES)
        def _(p):
            lanes = column(p)
            left = toep[b, pl.ds(p * 8, 8)].reshape(8 * SPAN, 2 * SPAN)
            big[...] = jnp.dot(left, xh[p, pl.ds(b * SPAN, 2 * SPAN), :], preferred_element_type=F32)
            group = lax.div(iota((SPAN, LANES), 1), 16)
            out = big[pl.ds(0, SPAN), :]
            for g in range(1, 8):
                out = jnp.where(group == g, big[pl.ds(g * SPAN, SPAN), :], out)
            rows = pl.ds(b * SPAN, SPAN)
            mixed[rows, lanes] = (gate[rows, lanes].astype(F32) * out).astype(BF16)

    convolve(1)
    upper, lower = pl.ds(0, SPAN), pl.ds(SPAN, SPAN)
    stores = [load(mixed.at[lower], mixed_out.at[lower], 12)]

    def states(e):
        arrived(abuf.at[0, 0, pl.ds(0, 192)], st_r.at[e])
        slot_sum[e] = (
            slot[e, 0].astype(F32) + slot_in[e, 1].astype(F32) + slot_in[e, 2].astype(F32) + slot_in[e, 3].astype(F32)
        ).astype(BF16)
        for pl_, pc in ((0, 0), (0, 1), (1, 0), (1, 1)):
            py = 2 * e + pl_
            dy, dc = lax.rem(py - y + 4, 4), lax.rem(pc - core + 2, 2)
            rows = pl.ds((pl_ * 2 + pc) * SPAN, SPAN)
            when_push(
                dy + dc > 0, slot_sum.at[e, rows], st.at[core * 4 + y], sy_s, sy_r.at[0],
                device(x, py, z, pc),
            )

            @pl.when(dy + dc == 0)
            def _():
                st[core * 4 + y] = slot_sum[e, rows, :]

    states(first_e)
    states(1 - first_e)
    for at_core, count in ((0, 128), (1, 112)):

        @pl.when(core == at_core)
        def _():
            arrived(abuf.at[0, 0, pl.ds(0, count)], hs_r.at[0])

    convolve(0)
    stores.append(load(mixed.at[upper], mixed_out.at[upper], 13))

    arrived(se_sin.at[pl.ds(1, 3)], sq_r.at[0])
    se_total = se_slot[0].astype(F32)
    for r in (1, 2, 3):
        se_total = se_total + se_sin[r].astype(F32)
    se_state[...] = se_total.astype(BF16)
    stores.append(load(se_state, se_out.at[0], 14))
    arrived(abuf.at[0, 0, pl.ds(0, 112)], sy_r.at[0])
    for p in range(8):
        mr_state[:, pl.ds(p * LANES, LANES)] = st[p]
    stores.append(load(mr_state, mr_out.at[0], 15))

    block = abuf.at[0, 0]
    for sem, ref in (
        (halo_s, halo), (ws_s, wq), (xs_s, wbuf.at[pl.ds(0, 2)]), (rl_s, wbuf.at[0]), (as_s, abuf.at[0]),
        (ar_s, block), (cf_s, abuf.at[pl.ds(0, 2)]), (k_s, block.at[pl.ds(0, 224)]), (zh_s, kp),
        (zs_s, cstage.at[0]), (fs_s, block.at[pl.ds(0, 224)]), (st_s, wbuf.at[0, pl.ds(0, 3)]),
        (sy_s, block.at[pl.ds(0, 112)]), (sp_s, block.at[pl.ds(0, 96)]), (sq_s, block.at[pl.ds(0, 48)]),
    ):
        remote(ref, ref, sem, sem, other).wait_send()
    for at_core, count in ((0, 128), (1, 112)):

        @pl.when(core == at_core)
        def _():
            ref = block.at[pl.ds(0, count)]
            remote(ref, ref, hs_s, hs_s, other).wait_send()

    for copy in stores:
        copy.wait()


def finish(mixed_in, se_in, mr_in, mixed, se_state, mr_state):
    mixed[...] = mixed_in[...]
    se_state[...] = se_in[:, pl.ds(0, TAPS - 1), :]
    mr_state[...] = mr_in[:, pl.ds(0, SPAN - 1), :]


def on_device(feats_se, filt_se, w_out, feats_mr, filt_mr, lengths, owners):
    vmem, anywhere = pl.BlockSpec(memory_space=pltpu.VMEM), pl.BlockSpec(memory_space=pl.ANY)
    dma = pltpu.SemaphoreType.DMA
    scratch = [
        pltpu.SMEM((8,), I32), pltpu.SMEM((8,), I32),
        pltpu.VMEM((TAPS, 64), F32), pltpu.VMEM((64, SPAN), F32),
        pltpu.VMEM((ROWS, WIDTH), BF16), pltpu.VMEM((16, WIDTH), BF16), pltpu.VMEM((SPAN, WIDTH), BF16),
        pltpu.VMEM((3, ROWS, WIDTH), BF16),
        pltpu.VMEM((2, 16, WIDTH), BF16),
        pltpu.VMEM((ROWS, WIDTH), BF16),
        pltpu.VMEM((4, 2, ROWS, LANES), BF16),
        pltpu.VMEM((2, 2, 2, ROWS, LANES), BF16),
        pltpu.VMEM((ROWS + 16, WIDTH), F32),
        pltpu.VMEM((ROWS, LANES), I32),
        pltpu.VMEM((3, WIDTH, LANES), BF16),
        pltpu.VMEM((4, 4, WIDTH, LANES), BF16),
        pltpu.VMEM((4, 2, ROWS, WIDTH), BF16),
        pltpu.VMEM((2, 4, 2, 2 * ROWS, LANES), BF16),
        pltpu.VMEM((2, 4, 2, ROWS, LANES), BF16),
        pltpu.VMEM((2, 2, 2, 2 * ROWS, LANES), BF16),
        pltpu.VMEM((2, 2, 2 * ROWS, LANES), BF16),
        pltpu.VMEM((64, SPAN), F32),
        pltpu.VMEM((2, 64, SPAN, 2 * SPAN), BF16),
        pltpu.VMEM((16, SPAN, 4 * ROWS), BF16),
        pltpu.VMEM((8, ROWS + SPAN, LANES), BF16),
        pltpu.VMEM((4, 4 * SPAN, LANES), F32),
        pltpu.VMEM((2, 4, 4 * SPAN, LANES), BF16),
        pltpu.VMEM((2, 4, 4 * SPAN, LANES), BF16),
        pltpu.VMEM((2, 4 * SPAN, LANES), BF16),
        pltpu.VMEM((8, SPAN, LANES), BF16),
        pltpu.VMEM((ROWS, WIDTH), BF16),
        pltpu.VMEM((4, 32, WIDTH), BF16),
        pltpu.VMEM((4, 32, WIDTH), BF16),
        pltpu.VMEM((4, 16, WIDTH), BF16),
        pltpu.VMEM((4, 16, WIDTH), BF16),
        pltpu.VMEM((8 * SPAN, LANES), F32),
        pltpu.VMEM((8, WIDTH), F32),
        dma((16,)), dma((16,)), dma((1,)), dma((3,)), dma((2, 4)), dma((1,)), dma((2, 2)), dma((2,)), dma((2,)),
        dma((1,)), dma((2, 4, 2)), dma((2, 2, 2)), dma((1,)), dma((1,)), dma((2,)), dma((1,)), dma((1,)), dma((1,)),
    ]
    results = pl.pallas_call(
        kernel,
        out_shape=(
            jax.ShapeDtypeStruct((ROWS, WIDTH), BF16),
            jax.ShapeDtypeStruct((1, 16, WIDTH), BF16),
            jax.ShapeDtypeStruct((1, SPAN, WIDTH), BF16),
        ),
        in_specs=[anywhere] * 7,
        out_specs=(anywhere, anywhere, anywhere),
        scratch_shapes=scratch,
        compiler_params=pltpu.CompilerParams(
            collective_id=0, has_side_effects=True, vmem_limit_bytes=56 * 2**20
        ),
        cost_estimate=pl.CostEstimate(flops=5 * 10**9, bytes_accessed=5 * 10**6, transcendentals=0),
        name="hyena",
    )(lengths, owners, filt_se.T, filt_mr, feats_se, w_out, feats_mr)
    return pl.pallas_call(
        finish,
        out_shape=(
            jax.ShapeDtypeStruct((ROWS, WIDTH), BF16),
            jax.ShapeDtypeStruct((1, TAPS - 1, WIDTH), BF16),
            jax.ShapeDtypeStruct((1, SPAN - 1, WIDTH), BF16),
        ),
        in_specs=[vmem] * 3,
        out_specs=(vmem, vmem, vmem),
        compiler_params=pltpu.CompilerParams(vmem_limit_bytes=56 * 2**20),
        name="outputs",
    )(*results)


def solution(mesh):
    in_specs = (
        P(None, "ctx", "chan"),
        P("chan", None),
        P("chan", "ctx"),
        P(None, "ctx", "chan"),
        P("chan", None),
        P(),
        P(),
    )
    out_specs = (P("ctx", "chan"), P("ctx", None, "chan"), P("ctx", None, "chan"))
    return jax.shard_map(
        on_device, mesh=mesh, in_specs=in_specs, out_specs=out_specs, check_vma=False
    )
```

```python
import jax
import jax.numpy as jnp
from jax import lax
from jax.experimental import pallas as pl
from jax.experimental.pallas import tpu as pltpu
from jax.sharding import PartitionSpec as P

BF16, F32, I32 = jnp.bfloat16, jnp.float32, jnp.int32
MESH = pl.DeviceIdType.MESH
ROWS, WIDTH, LANES = 256, 1024, 128
TAPS, SPAN = 7, 128
FAR = 1 << 20


def iota(shape, axis):
    return lax.broadcasted_iota(I32, shape, axis)


def kernel(
    lengths_in, owners_in, filt_se_in, filt_mr_in, feats_se, w_out, feats_mr,
    mixed_out, se_out, mr_out,
    lengths, owners, filt_se, filt_mr, mixed, se_state, mr_state,
    feat, gate, kp, kz, se_in, rel, wq, wbuf, abuf, cstage, zh, zbuf, red, g0, toep, pick,
    xh, slot_half, slot, slot_in, slot_sum, st, se_bf, se_part, se_pin, se_slot, se_sin, big, taps,
    load_sem, out_sem, halo_r, ws_r, xs_r, rl_r, as_r, ar_r, cf_r, k_r, zh_r, zs_r, fs_r, hs_r, st_r, sy_r, sp_r, sq_r,
):
    ctx, chan = lax.axis_index("ctx"), lax.axis_index("chan")
    core, x, low = lax.rem(ctx, 2), lax.rem(lax.div(ctx, 2), 4), lax.div(ctx, 8)
    high, z = lax.rem(chan, 2), lax.div(chan, 2)
    y = high * 2 + low

    def device(px, py, pz, pc):
        return {"ctx": lax.rem(py, 2) * 8 + px * 2 + pc, "chan": pz * 2 + lax.div(py, 2)}

    def near(dx, dy, dz, dc):
        return device(lax.rem(x + dx, 4), lax.rem(y + dy, 4), lax.rem(z + dz, 4), lax.rem(core + dc, 2))

    other = near(0, 0, 0, 1)
    partner = device(x, high * 2 + 1 - low, z, core)
    across = device(x, high * 2 + 1 - low, z, 1 - core)
    after, before = {"ctx": lax.rem(ctx + 1, 16)}, {"ctx": lax.rem(ctx + 15, 16)}

    def remote(src, dst, send, recv, to):
        return pltpu.make_async_remote_copy(
            src_ref=src, dst_ref=dst, send_sem=send, recv_sem=recv, device_id=to, device_id_type=MESH
        )

    (
        halo_s, ws_s, xs_s, rl_s, as_s, ar_s, cf_s, k_s, zh_s, zs_s, fs_s, hs_s, st_s, sy_s, sp_s, sq_s,
    ) = [out_sem.at[i] for i in range(16)]

    def push(src, dst, send, recv, to):
        remote(src, dst, send, recv, to).start()

    def arrived(ref, recv):
        remote(ref, ref, recv, recv, other).wait_recv()

    def load(src, dst, at):
        copy = pltpu.make_async_copy(src, dst, load_sem.at[at])
        copy.start()
        return copy

    def column(q):
        return pl.ds(pl.multiple_of(q * LANES, LANES), LANES)

    barrier = pltpu.get_barrier_semaphore()
    peers = [after, before]
    peers += [near(0, dy, 0, dc) for dy in range(4) for dc in range(2) if dy or dc]
    peers += [near(d, 0, 0, 0) for d in (1, 2, 3)] + [near(0, 0, d, 0) for d in (1, 2, 3)]
    for peer in peers:
        pl.semaphore_signal(barrier, inc=1, device_id=peer, device_id_type=MESH)

    @pl.when(core == 0)
    def _():
        for dy in range(4):
            for dc in range(2):
                pl.semaphore_signal(barrier, inc=1, device_id=near(3, dy, 0, dc), device_id_type=MESH)

    w_loads = [None] * 4
    for dy in (1, 3, 2, 0):
        src = w_out.at[:, column(lax.rem(y + dy, 4))]
        w_loads[dy] = load(src, wbuf.at[0, y] if dy == 0 else wq.at[dy - 1], dy)
    kv_load = load(feats_se.at[pl.ds(1, 2)], feat.at[pl.ds(1, 2)], 4)
    small = [load(lengths_in, lengths, 7), load(filt_se_in, filt_se, 9)]
    q_load = load(feats_se.at[0], feat.at[0], 5)
    late = [load(owners_in, owners, 8), load(filt_mr_in, filt_mr, 10)]
    gate_load = load(feats_mr.at[0], gate, 6)
    k_loads = []
    for dy in range(4):
        for dc in range(2):
            p = lax.rem(core + dc, 2) * 4 + lax.rem(y + dy, 4)
            dst = kp.at[dy, dc] if dy or dc else kz.at[high, low, core]
            k_loads.append(load(feats_mr.at[1, :, column(p)], dst, 11))

    pl.semaphore_wait(barrier, len(peers) + 4)

    kv_load.wait()
    tail = pl.ds(ROWS - 16, 16)
    se_in[pl.ds(ROWS + 8, 8), :] = (feat[1, tail, :].astype(F32) * feat[2, tail, :].astype(F32))[8:]
    edge_rows = se_in.at[pl.ds(8, 8)]
    push(se_in.at[pl.ds(ROWS + 8, 8)], edge_rows, halo_s, halo_r.at[0], after)
    for dy in (1, 3, 2):
        w_loads[dy].wait()
        push(wq.at[dy - 1], wbuf.at[0, y], ws_s, ws_r.at[dy - 1], near(0, dy, 0, 0))
    w_loads[0].wait()

    order = [y, lax.rem(y + 3, 4), lax.rem(y + 1, 4), lax.rem(y + 2, 4)]
    down, up, far = order[1], order[2], order[3]

    def spread(k):
        if k:
            arrived(wbuf.at[0, order[k]], ws_r.at[(0, 1, 3, 2)[k] - 1])
        push(wbuf.at[0, order[k]], wbuf.at[3, order[k]], xs_s, xs_r.at[0, k], near(1, 0, 0, 0))
        push(wbuf.at[0, order[k]], wbuf.at[1, order[k]], xs_s, xs_r.at[1, k], near(3, 0, 0, 0))

    def pass_on(k):
        half = WIDTH // 2
        first, second = pl.ds(0, half), pl.ds(half, half)
        arrived(wbuf.at[3, order[k]], xs_r.at[0, k])
        push(wbuf.at[3, order[k], first], wbuf.at[2, order[k], first], rl_s, rl_r.at[0], near(1, 0, 0, 0))
        arrived(wbuf.at[1, order[k]], xs_r.at[1, k])
        push(wbuf.at[1, order[k], second], wbuf.at[2, order[k], second], rl_s, rl_r.at[0], near(3, 0, 0, 0))

    spread(0)

    for copy in small:
        copy.wait()
    starts, ends = [], []
    total = jnp.int32(0)
    for r in range(8):
        starts.append(total)
        total = total + lengths[r]
        ends.append(total)
    pos = iota((ROWS, LANES), 0) + ctx * ROWS
    seg = jnp.zeros((ROWS, LANES), I32)
    for r in range(8):
        seg = jnp.maximum(seg, jnp.where(starts[r] <= pos, starts[r], 0))
    rel[...] = pos - seg

    spread_out = jnp.where(lax.div(iota((64, WIDTH), 1), 16) == iota((64, WIDTH), 0), 1.0, 0.0).astype(F32)
    taps[pl.ds(0, TAPS), :] = lax.dot_general(
        filt_se[...], spread_out, (((1,), (0,)), ((), ())),
        precision=lax.Precision.HIGHEST, preferred_element_type=F32,
    )
    product_in = feat[1].astype(F32) * feat[2].astype(F32)
    se_in[pl.ds(16, ROWS - 8), :] = product_in[: ROWS - 8]
    se_bf[...] = product_in.astype(BF16)
    q_load.wait()

    def short(first, count):
        @pl.loop(0, WIDTH // LANES)
        def _(p):
            lanes = column(p)
            acc = jnp.zeros((count, LANES), F32)
            for j in range(TAPS):
                term = taps[pl.ds(j, 1), lanes] * se_in[pl.ds(16 + first - j, count), lanes]
                acc = acc + jnp.where(rel[pl.ds(first, count), :] >= j, term, 0.0)
            rows = pl.ds(first, count)
            abuf[y, core, rows, lanes] = (feat[0, rows, lanes].astype(F32) * acc).astype(BF16)

    short(16, ROWS - 16)
    arrived(edge_rows, halo_r.at[0])
    short(0, 16)

    half = pl.ds(0, ROWS // 2), pl.ds(ROWS // 2, ROWS // 2)
    for i in range(2):
        for way in range(2):
            mine = abuf.at[y, core, half[i ^ way]]
            push(mine, mine, as_s, as_r.at[way, i], near(0, (1, 3)[way], 0, 0))
    mine = abuf.at[y, core]
    push(mine, mine, cf_s, cf_r.at[0], other)

    for copy in late:
        copy.wait()

    def request_at(target):
        end = jnp.int32(-FAR)
        start = jnp.int32(0)
        for r in range(8):
            end = jnp.where(owners[r] == target, ends[r], end)
            start = jnp.where(owners[r] == target, starts[r], start)
        return end, start

    def picker(end, start, base, span, rows):
        at = iota((rows, ROWS), 1) + base
        row = iota((rows, ROWS), 0)
        keep = (at == end - span + row) & (at >= start) & (row < span)
        return jnp.where(keep, 1.0, 0.0).astype(BF16)

    groups = [(low, core), (low, 1 - core), (1 - low, core), (1 - low, 1 - core)]
    for g, (to_low, to_core) in enumerate(groups):
        rows = []
        for r in range(4):
            end, start = request_at(to_low * 8 + lax.rem(x + r, 4) * 2 + to_core)
            rows.append(picker(end, start, ctx * ROWS, TAPS - 1, 8))
        se_part[g] = jnp.dot(
            jnp.concatenate(rows, axis=0), se_bf[...], preferred_element_type=F32
        ).astype(BF16)

    spread(1)
    spread(2)

    turn = jnp.where(lax.rem(iota((SPAN, SPAN), 0) + iota((SPAN, SPAN), 1), SPAN) == 0, 1.0, 0.0)
    g0[...] = jnp.dot(filt_mr[...].astype(BF16), turn.astype(BF16), preferred_element_type=F32)

    def band(first, count):
        @pl.loop(first, first + count)
        def _(g):
            ring = pltpu.roll(
                jnp.broadcast_to(g0[pl.ds(g, 1), :], (SPAN, SPAN)), 0, 1, stride=1, stride_axis=0
            )
            step = iota((SPAN, SPAN), 0) - iota((SPAN, SPAN), 1)
            for b in range(2):
                reach = rel[pl.ds(b * SPAN, SPAN), :]
                left = jnp.where((step < 0) & (step + SPAN <= reach), ring, 0.0)
                right = jnp.where((step >= 0) & (step <= reach), ring, 0.0)
                toep[b, g, :, pl.ds(0, SPAN)] = left.astype(BF16)
                toep[b, g, :, pl.ds(SPAN, SPAN)] = right.astype(BF16)

    band(0, 24)
    pass_on(0)
    spread(3)
    band(24, 40)

    @pl.loop(0, 16)
    def _(i):
        target = lax.rem(lax.div(i, 2), 2) * 8 + lax.rem(x + lax.div(i, 4), 4) * 2 + lax.rem(i, 2)
        end, start = request_at(target)
        for b in range(4):
            base = ((b // 2) * 8 + x * 2 + b % 2) * ROWS
            pick[i, :, pl.ds(b * ROWS, ROWS)] = picker(end, start, base, SPAN - 1, SPAN)

    pass_on(1)
    pass_on(2)
    def to_core(block, part, at):
        push(abuf.at[block, core, part], abuf.at[block, core, part], cf_s, cf_r.at[at], other)

    arrived(abuf.at[down, core, half[0]], as_r.at[0, 0])
    push(abuf.at[down, core, half[0]], abuf.at[down, core, half[0]], ar_s, ar_r.at[0], near(0, 1, 0, 0))
    to_core(down, half[0], 0)
    arrived(abuf.at[up, core, half[1]], as_r.at[1, 0])
    push(abuf.at[up, core, half[1]], abuf.at[up, core, half[1]], ar_s, ar_r.at[1], near(0, 3, 0, 0))
    to_core(up, half[1], 0)
    arrived(abuf.at[down, core, half[1]], as_r.at[0, 1])
    to_core(down, half[1], 0)
    arrived(abuf.at[up, core, half[0]], as_r.at[1, 1])
    to_core(up, half[0], 0)

    def when_push(cond, src, dst, send, recv, to):
        @pl.when(cond)
        def _():
            push(src, dst, send, recv, to)

    lo, hi = pl.ds(0, ROWS), pl.ds(ROWS, ROWS)
    above, below = near(0, 0, 1, 0), near(0, 0, 3, 0)
    to_above, to_below = lax.div(lax.rem(z + 1, 4), 2), lax.div(lax.rem(z + 3, 4), 2)

    def same_side(r):
        return lax.div(lax.rem(x + r, 4), 2) == lax.rem(z, 2)

    def product(tl, r, blocks):
        acc = None
        for hh in range(2):
            right = jnp.concatenate([wbuf[r, 2 * hh], wbuf[r, 2 * hh + 1]], axis=1)
            part = jnp.dot(blocks(2 * hh + (low if tl == 0 else 1 - low)), right, preferred_element_type=F32)
            acc = part if acc is None else acc + part
        return acc

    def half_copy(tl, r, cc):
        rows = pl.ds(pl.multiple_of(cc * ROWS, ROWS), ROWS)
        return remote(
            cstage.at[tl, r, 1 - lax.div(z, 2), rows], zh.at[tl, r, cc], zh_s, zh_r.at[tl, r, cc],
            near(0, 0, 1 + 2 * cc, 0),
        )

    def tasks(tl, turns, ready=None):
        @pl.loop(0, 2)
        def _(i):
            cc = lax.rem(core + i, 2)

            if ready is not None:

                @pl.when(i == 1)
                def _():
                    ready()

            for r in turns:
                acc = product(tl, r, lambda block: abuf[block, cc])
                rows = pl.ds(pl.multiple_of(cc * ROWS, ROWS), ROWS)
                cstage[tl, r, 0, rows, :] = acc[:, :LANES].astype(BF16)
                cstage[tl, r, 1, rows, :] = acc[:, LANES:].astype(BF16)

                @pl.when(same_side(r))
                def _():
                    half_copy(tl, r, cc).start()

    def add_on(tl, r):
        other_side = jnp.logical_not(same_side(r))
        e = lax.rem(lax.rem(x + r, 4), 2)

        @pl.when(other_side)
        def _():
            arrived(zh.at[tl, r, 0], zh_r.at[tl, r, 0])
            mine = cstage[tl, r, to_above, lo, :].astype(F32)
            cstage[tl, r, to_above, lo, :] = (mine + zh[tl, r, 0].astype(F32)).astype(BF16)

        when_push(
            other_side, cstage.at[tl, r, to_above], zbuf.at[0, tl, e], zs_s, zs_r.at[0, tl, e], above
        )

        @pl.when(other_side)
        def _():
            arrived(zh.at[tl, r, 1], zh_r.at[tl, r, 1])
            mine = cstage[tl, r, to_below, hi, :].astype(F32)
            cstage[tl, r, to_below, hi, :] = (mine + zh[tl, r, 1].astype(F32)).astype(BF16)

        when_push(
            other_side, cstage.at[tl, r, to_below], zbuf.at[1, tl, e], zs_s, zs_r.at[1, tl, e], below
        )

    def near_ready():
        arrived(feat, cf_r.at[0])

    tasks(1, (0,), near_ready)
    pass_on(3)
    tasks(1, (1,))
    add_on(1, 0)
    tasks(1, (3,))
    arrived(abuf.at[far, core, half[0]], ar_r.at[0])
    to_core(far, half[0], 1)
    arrived(abuf.at[far, core, half[1]], ar_r.at[1])
    to_core(far, half[1], 1)
    pltpu.make_async_copy(kp, kp, load_sem.at[11]).wait()
    for dy in range(4):
        for dc in range(2):
            if dy or dc:
                push(kp.at[dy, dc], kz.at[high, low, core], k_s, k_r.at[0], near(0, dy, 0, dc))

    for g, to in ((1, other), (2, partner), (3, across)):
        push(se_part.at[g], se_pin.at[g], sp_s, sp_r.at[0], to)

    def far_ready():
        arrived(abuf.at[far, 1 - core], cf_r.at[1])

    tasks(0, (0,), far_ready)
    add_on(1, 1)
    tasks(0, (1,))
    add_on(1, 3)
    tasks(0, (3,))

    arrived(wbuf.at[2], rl_r.at[0])
    tasks(1, (2,))
    tasks(0, (2,))
    for add_tl, add_r in ((0, 0), (0, 1), (0, 3), (1, 2), (0, 2)):
        add_on(add_tl, add_r)

    arrived(abuf.at[0, 0, pl.ds(0, 224)], k_r.at[0])

    own_x = lax.rem(z, 2) * 2
    first_e = jnp.where(lax.rem(own_x - x + 4, 4) == 2, 1, 0)
    for e in (first_e, 1 - first_e):
        for tl in (1, 0):
            token_low = low if tl == 0 else 1 - low
            total = cstage[tl, lax.rem(own_x + e - x + 4, 4), lax.div(z, 2)].astype(F32)
            for way in range(2):
                arrived(zbuf.at[way, tl, e], zs_r.at[way, tl, e])
                total = total + zbuf[way, tl, e].astype(F32)
            total = total.astype(BF16).astype(F32)
            for cc in range(2):
                rows = slice(cc * ROWS, (cc + 1) * ROWS)
                value = kz[e, token_low, cc].astype(F32) * total[rows]
                red[e, token_low, pl.ds(cc * ROWS, ROWS), :] = value.astype(BF16)
            for pc in range(2):
                py = 2 * e + token_low
                dy, dc = lax.rem(py - y + 4, 4), lax.rem(pc - core + 2, 2)
                src = red.at[e, token_low, pl.ds(pc * ROWS, ROWS)]
                dst = xh.at[core * 4 + y, pl.ds(SPAN, ROWS)]
                when_push(dy + dc > 0, src, dst, fs_s, fs_r.at[0], device(x, py, z, pc))

                @pl.when(dy + dc == 0)
                def _():
                    xh[core * 4 + y, pl.ds(SPAN, ROWS), :] = red[e, token_low, pl.ds(pc * ROWS, ROWS), :]

            right = red[e, token_low]
            lanes = pl.ds(pl.multiple_of(token_low * 2 * ROWS, 2 * ROWS), 2 * ROWS)
            for r in (2, 1, 3, 0):
                left = pick[pl.ds(r * 4, 4), :, lanes].reshape(4 * SPAN, 2 * ROWS)
                some = jnp.dot(left, right, preferred_element_type=F32)
                if tl == 1:
                    slot_half[r] = some
                    continue
                slot[e, r] = (slot_half[r] + some).astype(BF16)
                if r:
                    push(slot.at[e, r], slot_in.at[e, r], st_s, st_r.at[e], near(r, 0, 0, 0))

    for e in range(2):
        for token_low in range(2):
            for pc in range(2):
                py = 2 * e + token_low
                last = red.at[e, token_low, pl.ds(pc * ROWS + SPAN, SPAN)]
                edge = xh.at[core * 4 + y, pl.ds(0, SPAN)]
                if pc == 0:
                    following = device(x, py, z, 1)
                    away = (py != y) | (core == 0)
                else:
                    wrap = lax.div(x, 3)
                    next_low = token_low + wrap - 2 * token_low * wrap
                    following = device(lax.rem(x + 1, 4), 2 * e + next_low, z, 0)
                    away = core >= 0
                at = token_low * 2 + pc
                when_push(away, last, edge, hs_s, hs_r.at[0], following)
                if pc == 0:

                    @pl.when(jnp.logical_not(away))
                    def _():
                        xh[core * 4 + y, pl.ds(0, SPAN), :] = red[e, token_low, pl.ds(SPAN, SPAN), :]

    arrived(se_pin.at[pl.ds(1, 3)], sp_r.at[0])
    se_sum = se_part[0].astype(F32) + se_pin[1].astype(F32) + se_pin[2].astype(F32) + se_pin[3].astype(F32)
    for r in range(4):
        rows = se_sum[8 * r : 8 * r + 8]
        se_slot[r] = jnp.concatenate([rows, jnp.zeros_like(rows)], axis=0).astype(BF16)
        if r:
            push(se_slot.at[r], se_sin.at[r], sq_s, sq_r.at[0], near(r, 0, 0, 0))

    arrived(abuf.at[0, 0, pl.ds(0, 224)], fs_r.at[0])
    gate_load.wait()

    def convolve(b):
        @pl.loop(0, WIDTH // LANES)
        def _(p):
            lanes = column(p)
            left = toep[b, pl.ds(p * 8, 8)].reshape(8 * SPAN, 2 * SPAN)
            big[...] = jnp.dot(left, xh[p, pl.ds(b * SPAN, 2 * SPAN), :], preferred_element_type=F32)
            group = lax.div(iota((SPAN, LANES), 1), 16)
            out = big[pl.ds(0, SPAN), :]
            for g in range(1, 8):
                out = jnp.where(group == g, big[pl.ds(g * SPAN, SPAN), :], out)
            rows = pl.ds(b * SPAN, SPAN)
            mixed[rows, lanes] = (gate[rows, lanes].astype(F32) * out).astype(BF16)

    convolve(1)
    upper, lower = pl.ds(0, SPAN), pl.ds(SPAN, SPAN)
    stores = [load(mixed.at[lower], mixed_out.at[lower], 12)]

    def states(e):
        arrived(abuf.at[0, 0, pl.ds(0, 192)], st_r.at[e])
        slot_sum[e] = (
            slot[e, 0].astype(F32) + slot_in[e, 1].astype(F32) + slot_in[e, 2].astype(F32) + slot_in[e, 3].astype(F32)
        ).astype(BF16)
        for pl_, pc in ((0, 0), (0, 1), (1, 0), (1, 1)):
            py = 2 * e + pl_
            dy, dc = lax.rem(py - y + 4, 4), lax.rem(pc - core + 2, 2)
            rows = pl.ds((pl_ * 2 + pc) * SPAN, SPAN)
            when_push(
                dy + dc > 0, slot_sum.at[e, rows], st.at[core * 4 + y], sy_s, sy_r.at[0],
                device(x, py, z, pc),
            )

            @pl.when(dy + dc == 0)
            def _():
                st[core * 4 + y] = slot_sum[e, rows, :]

    states(first_e)
    states(1 - first_e)
    for at_core, count in ((0, 128), (1, 112)):

        @pl.when(core == at_core)
        def _():
            arrived(abuf.at[0, 0, pl.ds(0, count)], hs_r.at[0])

    convolve(0)
    stores.append(load(mixed.at[upper], mixed_out.at[upper], 13))

    arrived(se_sin.at[pl.ds(1, 3)], sq_r.at[0])
    se_total = se_slot[0].astype(F32)
    for r in (1, 2, 3):
        se_total = se_total + se_sin[r].astype(F32)
    se_state[...] = se_total.astype(BF16)
    stores.append(load(se_state, se_out.at[0], 14))
    arrived(abuf.at[0, 0, pl.ds(0, 112)], sy_r.at[0])
    for p in range(8):
        mr_state[:, pl.ds(p * LANES, LANES)] = st[p]
    stores.append(load(mr_state, mr_out.at[0], 15))

    block = abuf.at[0, 0]
    for sem, ref in (
        (halo_s, edge_rows), (ws_s, wq), (xs_s, wbuf.at[pl.ds(0, 2)]), (rl_s, wbuf.at[0]), (as_s, abuf.at[0]),
        (ar_s, block), (cf_s, abuf.at[pl.ds(0, 2)]), (k_s, block.at[pl.ds(0, 224)]), (zh_s, kp),
        (zs_s, cstage.at[0]), (fs_s, block.at[pl.ds(0, 224)]), (st_s, wbuf.at[0, pl.ds(0, 3)]),
        (sy_s, block.at[pl.ds(0, 112)]), (sp_s, block.at[pl.ds(0, 96)]), (sq_s, block.at[pl.ds(0, 48)]),
    ):
        remote(ref, ref, sem, sem, other).wait_send()
    for at_core, count in ((0, 128), (1, 112)):

        @pl.when(core == at_core)
        def _():
            ref = block.at[pl.ds(0, count)]
            remote(ref, ref, hs_s, hs_s, other).wait_send()

    for copy in stores:
        copy.wait()


def finish(mixed_in, se_in, mr_in, mixed, se_state, mr_state):
    mixed[...] = mixed_in[...]
    se_state[...] = se_in[:, pl.ds(0, TAPS - 1), :]
    mr_state[...] = mr_in[:, pl.ds(0, SPAN - 1), :]


def on_device(feats_se, filt_se, w_out, feats_mr, filt_mr, lengths, owners):
    vmem, anywhere = pl.BlockSpec(memory_space=pltpu.VMEM), pl.BlockSpec(memory_space=pl.ANY)
    dma = pltpu.SemaphoreType.DMA
    scratch = [
        pltpu.SMEM((8,), I32), pltpu.SMEM((8,), I32),
        pltpu.VMEM((TAPS, 64), F32), pltpu.VMEM((64, SPAN), F32),
        pltpu.VMEM((ROWS, WIDTH), BF16), pltpu.VMEM((16, WIDTH), BF16), pltpu.VMEM((SPAN, WIDTH), BF16),
        pltpu.VMEM((3, ROWS, WIDTH), BF16),
        pltpu.VMEM((ROWS, WIDTH), BF16),
        pltpu.VMEM((4, 2, ROWS, LANES), BF16),
        pltpu.VMEM((2, 2, 2, ROWS, LANES), BF16),
        pltpu.VMEM((ROWS + 16, WIDTH), F32),
        pltpu.VMEM((ROWS, LANES), I32),
        pltpu.VMEM((3, WIDTH, LANES), BF16),
        pltpu.VMEM((4, 4, WIDTH, LANES), BF16),
        pltpu.VMEM((4, 2, ROWS, WIDTH), BF16),
        pltpu.VMEM((2, 4, 2, 2 * ROWS, LANES), BF16),
        pltpu.VMEM((2, 4, 2, ROWS, LANES), BF16),
        pltpu.VMEM((2, 2, 2, 2 * ROWS, LANES), BF16),
        pltpu.VMEM((2, 2, 2 * ROWS, LANES), BF16),
        pltpu.VMEM((64, SPAN), F32),
        pltpu.VMEM((2, 64, SPAN, 2 * SPAN), BF16),
        pltpu.VMEM((16, SPAN, 4 * ROWS), BF16),
        pltpu.VMEM((8, ROWS + SPAN, LANES), BF16),
        pltpu.VMEM((4, 4 * SPAN, LANES), F32),
        pltpu.VMEM((2, 4, 4 * SPAN, LANES), BF16),
        pltpu.VMEM((2, 4, 4 * SPAN, LANES), BF16),
        pltpu.VMEM((2, 4 * SPAN, LANES), BF16),
        pltpu.VMEM((8, SPAN, LANES), BF16),
        pltpu.VMEM((ROWS, WIDTH), BF16),
        pltpu.VMEM((4, 32, WIDTH), BF16),
        pltpu.VMEM((4, 32, WIDTH), BF16),
        pltpu.VMEM((4, 16, WIDTH), BF16),
        pltpu.VMEM((4, 16, WIDTH), BF16),
        pltpu.VMEM((8 * SPAN, LANES), F32),
        pltpu.VMEM((8, WIDTH), F32),
        dma((16,)), dma((16,)), dma((1,)), dma((3,)), dma((2, 4)), dma((1,)), dma((2, 2)), dma((2,)), dma((2,)),
        dma((1,)), dma((2, 4, 2)), dma((2, 2, 2)), dma((1,)), dma((1,)), dma((2,)), dma((1,)), dma((1,)), dma((1,)),
    ]
    results = pl.pallas_call(
        kernel,
        out_shape=(
            jax.ShapeDtypeStruct((ROWS, WIDTH), BF16),
            jax.ShapeDtypeStruct((1, 16, WIDTH), BF16),
            jax.ShapeDtypeStruct((1, SPAN, WIDTH), BF16),
        ),
        in_specs=[anywhere] * 7,
        out_specs=(anywhere, anywhere, anywhere),
        scratch_shapes=scratch,
        compiler_params=pltpu.CompilerParams(
            collective_id=0, has_side_effects=True, vmem_limit_bytes=56 * 2**20
        ),
        cost_estimate=pl.CostEstimate(flops=5 * 10**9, bytes_accessed=5 * 10**6, transcendentals=0),
        name="hyena",
    )(lengths, owners, filt_se.T, filt_mr, feats_se, w_out, feats_mr)
    return pl.pallas_call(
        finish,
        out_shape=(
            jax.ShapeDtypeStruct((ROWS, WIDTH), BF16),
            jax.ShapeDtypeStruct((1, TAPS - 1, WIDTH), BF16),
            jax.ShapeDtypeStruct((1, SPAN - 1, WIDTH), BF16),
        ),
        in_specs=[vmem] * 3,
        out_specs=(vmem, vmem, vmem),
        compiler_params=pltpu.CompilerParams(vmem_limit_bytes=56 * 2**20),
        name="outputs",
    )(*results)


def solution(mesh):
    in_specs = (
        P(None, "ctx", "chan"),
        P("chan", None),
        P("chan", "ctx"),
        P(None, "ctx", "chan"),
        P("chan", None),
        P(),
        P(),
    )
    out_specs = (P("ctx", "chan"), P("ctx", None, "chan"), P("ctx", None, "chan"))
    return jax.shard_map(
        on_device, mesh=mesh, in_specs=in_specs, out_specs=out_specs, check_vma=False
    )
```

```python
import jax
import jax.numpy as jnp
from jax import lax
from jax.experimental import pallas as pl
from jax.experimental.pallas import tpu as pltpu
from jax.sharding import PartitionSpec as P

BF16, F32, I32 = jnp.bfloat16, jnp.float32, jnp.int32
MESH = pl.DeviceIdType.MESH
ROWS, WIDTH, LANES = 256, 1024, 128
TAPS, SPAN = 7, 128
FAR = 1 << 20


def iota(shape, axis):
    return lax.broadcasted_iota(I32, shape, axis)


def kernel(
    lengths_in, owners_in, filt_se_in, filt_mr_in, feats_se, w_out, feats_mr,
    mixed_out, se_out, mr_out,
    lengths, owners, filt_se, filt_mr, mixed, se_state, mr_state,
    feat, halo, gate, kp, kz, se_in, rel, wq, wbuf, abuf, cstage, zh, zbuf, red, g0, toep, pick,
    xh, slot_half, slot, slot_in, slot_sum, st, se_bf, se_part, se_pin, se_slot, se_sin, big, taps,
    load_sem, out_sem, halo_r, ws_r, xs_r, rl_r, as_r, ar_r, cf_r, k_r, zh_r, zs_r, fs_r, hs_r, st_r, sy_r, sp_r, sq_r,
):
    ctx, chan = lax.axis_index("ctx"), lax.axis_index("chan")
    core, x, low = lax.rem(ctx, 2), lax.rem(lax.div(ctx, 2), 4), lax.div(ctx, 8)
    high, z = lax.rem(chan, 2), lax.div(chan, 2)
    y = high * 2 + low

    def device(px, py, pz, pc):
        return {"ctx": lax.rem(py, 2) * 8 + px * 2 + pc, "chan": pz * 2 + lax.div(py, 2)}

    def near(dx, dy, dz, dc):
        return device(lax.rem(x + dx, 4), lax.rem(y + dy, 4), lax.rem(z + dz, 4), lax.rem(core + dc, 2))

    other = near(0, 0, 0, 1)
    partner = device(x, high * 2 + 1 - low, z, core)
    across = device(x, high * 2 + 1 - low, z, 1 - core)
    after, before = {"ctx": lax.rem(ctx + 1, 16)}, {"ctx": lax.rem(ctx + 15, 16)}

    def remote(src, dst, send, recv, to):
        return pltpu.make_async_remote_copy(
            src_ref=src, dst_ref=dst, send_sem=send, recv_sem=recv, device_id=to, device_id_type=MESH
        )

    (
        halo_s, ws_s, xs_s, rl_s, as_s, ar_s, cf_s, k_s, zh_s, zs_s, fs_s, hs_s, st_s, sy_s, sp_s, sq_s,
    ) = [out_sem.at[i] for i in range(16)]

    def push(src, dst, send, recv, to):
        remote(src, dst, send, recv, to).start()

    def arrived(ref, recv):
        remote(ref, ref, recv, recv, other).wait_recv()

    def load(src, dst, at):
        copy = pltpu.make_async_copy(src, dst, load_sem.at[at])
        copy.start()
        return copy

    def column(q):
        return pl.ds(pl.multiple_of(q * LANES, LANES), LANES)

    barrier = pltpu.get_barrier_semaphore()
    peers = [after, before]
    peers += [near(0, dy, 0, dc) for dy in range(4) for dc in range(2) if dy or dc]
    peers += [near(d, 0, 0, 0) for d in (1, 2, 3)] + [near(0, 0, d, 0) for d in (1, 2, 3)]
    for peer in peers:
        pl.semaphore_signal(barrier, inc=1, device_id=peer, device_id_type=MESH)

    @pl.when(core == 0)
    def _():
        for dy in range(4):
            for dc in range(2):
                pl.semaphore_signal(barrier, inc=1, device_id=near(3, dy, 0, dc), device_id_type=MESH)

    w_loads = [None] * 4
    for dy in (1, 3, 2, 0):
        src = w_out.at[:, column(lax.rem(y + dy, 4))]
        w_loads[dy] = load(src, wbuf.at[0, y] if dy == 0 else wq.at[dy - 1], dy)
    kv_load = load(feats_se.at[pl.ds(1, 2)], feat.at[pl.ds(1, 2)], 4)
    small = [load(lengths_in, lengths, 7), load(filt_se_in, filt_se, 9)]
    q_load = load(feats_se.at[0], feat.at[0], 5)
    late = [load(owners_in, owners, 8), load(filt_mr_in, filt_mr, 10)]
    gate_load = load(feats_mr.at[0], gate, 6)
    k_loads = []
    for dy in range(4):
        for dc in range(2):
            p = lax.rem(core + dc, 2) * 4 + lax.rem(y + dy, 4)
            dst = kp.at[dy, dc] if dy or dc else kz.at[high, low, core]
            k_loads.append(load(feats_mr.at[1, :, column(p)], dst, 11))

    pl.semaphore_wait(barrier, len(peers) + 4)

    push(feats_se.at[pl.ds(1, 2), pl.ds(ROWS - 16, 16)], halo, halo_s, halo_r.at[0], after)
    for dy in (1, 3, 2):
        w_loads[dy].wait()
        push(wq.at[dy - 1], wbuf.at[0, y], ws_s, ws_r.at[dy - 1], near(0, dy, 0, 0))
    w_loads[0].wait()

    order = [y, lax.rem(y + 3, 4), lax.rem(y + 1, 4), lax.rem(y + 2, 4)]
    down, up, far = order[1], order[2], order[3]

    def spread(k):
        if k:
            arrived(wbuf.at[0, order[k]], ws_r.at[(0, 1, 3, 2)[k] - 1])
        push(wbuf.at[0, order[k]], wbuf.at[3, order[k]], xs_s, xs_r.at[0, k], near(1, 0, 0, 0))
        push(wbuf.at[0, order[k]], wbuf.at[1, order[k]], xs_s, xs_r.at[1, k], near(3, 0, 0, 0))

    def pass_on(k):
        half = WIDTH // 2
        first, second = pl.ds(0, half), pl.ds(half, half)
        arrived(wbuf.at[3, order[k]], xs_r.at[0, k])
        push(wbuf.at[3, order[k], first], wbuf.at[2, order[k], first], rl_s, rl_r.at[0], near(1, 0, 0, 0))
        arrived(wbuf.at[1, order[k]], xs_r.at[1, k])
        push(wbuf.at[1, order[k], second], wbuf.at[2, order[k], second], rl_s, rl_r.at[0], near(3, 0, 0, 0))

    spread(0)

    for copy in small:
        copy.wait()
    starts, ends = [], []
    total = jnp.int32(0)
    for r in range(8):
        starts.append(total)
        total = total + lengths[r]
        ends.append(total)
    pos = iota((ROWS, LANES), 0) + ctx * ROWS
    seg = jnp.zeros((ROWS, LANES), I32)
    for r in range(8):
        seg = jnp.maximum(seg, jnp.where(starts[r] <= pos, starts[r], 0))
    rel[...] = pos - seg

    spread_out = jnp.where(lax.div(iota((64, WIDTH), 1), 16) == iota((64, WIDTH), 0), 1.0, 0.0).astype(F32)
    taps[pl.ds(0, TAPS), :] = lax.dot_general(
        filt_se[...], spread_out, (((1,), (0,)), ((), ())),
        precision=lax.Precision.HIGHEST, preferred_element_type=F32,
    )
    kv_load.wait()
    se_in[pl.ds(16, ROWS), :] = feat[1].astype(F32) * feat[2].astype(F32)
    se_bf[...] = se_in[pl.ds(16, ROWS), :].astype(BF16)
    q_load.wait()

    def short(first, count):
        @pl.loop(0, WIDTH // LANES)
        def _(p):
            lanes = column(p)
            acc = jnp.zeros((count, LANES), F32)
            for j in range(TAPS):
                term = taps[pl.ds(j, 1), lanes] * se_in[pl.ds(16 + first - j, count), lanes]
                acc = acc + jnp.where(rel[pl.ds(first, count), :] >= j, term, 0.0)
            rows = pl.ds(first, count)
            abuf[y, core, rows, lanes] = (feat[0, rows, lanes].astype(F32) * acc).astype(BF16)

    short(16, ROWS - 16)
    arrived(halo, halo_r.at[0])
    se_in[pl.ds(0, 16), :] = halo[0].astype(F32) * halo[1].astype(F32)
    short(0, 16)

    half = pl.ds(0, ROWS // 2), pl.ds(ROWS // 2, ROWS // 2)
    for i in range(2):
        for way in range(2):
            mine = abuf.at[y, core, half[i ^ way]]
            push(mine, mine, as_s, as_r.at[way, i], near(0, (1, 3)[way], 0, 0))
    mine = abuf.at[y, core]
    push(mine, mine, cf_s, cf_r.at[0], other)

    for copy in late:
        copy.wait()

    def request_at(target):
        end = jnp.int32(-FAR)
        start = jnp.int32(0)
        for r in range(8):
            end = jnp.where(owners[r] == target, ends[r], end)
            start = jnp.where(owners[r] == target, starts[r], start)
        return end, start

    def picker(end, start, base, span, rows):
        at = iota((rows, ROWS), 1) + base
        row = iota((rows, ROWS), 0)
        keep = (at == end - span + row) & (at >= start) & (row < span)
        return jnp.where(keep, 1.0, 0.0).astype(BF16)

    groups = [(low, core), (low, 1 - core), (1 - low, core), (1 - low, 1 - core)]
    for g, (to_low, to_core) in enumerate(groups):
        rows = []
        for r in range(4):
            end, start = request_at(to_low * 8 + lax.rem(x + r, 4) * 2 + to_core)
            rows.append(picker(end, start, ctx * ROWS, TAPS - 1, 8))
        se_part[g] = jnp.dot(
            jnp.concatenate(rows, axis=0), se_bf[...], preferred_element_type=F32
        ).astype(BF16)

    spread(1)
    spread(2)

    turn = jnp.where(lax.rem(iota((SPAN, SPAN), 0) + iota((SPAN, SPAN), 1), SPAN) == 0, 1.0, 0.0)
    g0[...] = jnp.dot(filt_mr[...].astype(BF16), turn.astype(BF16), preferred_element_type=F32)

    def band(first, count):
        @pl.loop(first, first + count)
        def _(g):
            ring = pltpu.roll(
                jnp.broadcast_to(g0[pl.ds(g, 1), :], (SPAN, SPAN)), 0, 1, stride=1, stride_axis=0
            )
            step = iota((SPAN, SPAN), 0) - iota((SPAN, SPAN), 1)
            for b in range(2):
                reach = rel[pl.ds(b * SPAN, SPAN), :]
                left = jnp.where((step < 0) & (step + SPAN <= reach), ring, 0.0)
                right = jnp.where((step >= 0) & (step <= reach), ring, 0.0)
                toep[b, g, :, pl.ds(0, SPAN)] = left.astype(BF16)
                toep[b, g, :, pl.ds(SPAN, SPAN)] = right.astype(BF16)

    band(0, 24)
    pass_on(0)
    spread(3)
    band(24, 40)

    @pl.loop(0, 16)
    def _(i):
        target = lax.rem(lax.div(i, 2), 2) * 8 + lax.rem(x + lax.div(i, 4), 4) * 2 + lax.rem(i, 2)
        end, start = request_at(target)
        for b in range(4):
            base = ((b // 2) * 8 + x * 2 + b % 2) * ROWS
            pick[i, :, pl.ds(b * ROWS, ROWS)] = picker(end, start, base, SPAN - 1, SPAN)

    pass_on(1)
    pass_on(2)
    def to_core(block, part, at):
        push(abuf.at[block, core, part], abuf.at[block, core, part], cf_s, cf_r.at[at], other)

    arrived(abuf.at[down, core, half[0]], as_r.at[0, 0])
    push(abuf.at[down, core, half[0]], abuf.at[down, core, half[0]], ar_s, ar_r.at[0], near(0, 1, 0, 0))
    to_core(down, half[0], 0)
    arrived(abuf.at[up, core, half[1]], as_r.at[1, 0])
    push(abuf.at[up, core, half[1]], abuf.at[up, core, half[1]], ar_s, ar_r.at[1], near(0, 3, 0, 0))
    to_core(up, half[1], 0)
    arrived(abuf.at[down, core, half[1]], as_r.at[0, 1])
    to_core(down, half[1], 0)
    arrived(abuf.at[up, core, half[0]], as_r.at[1, 1])
    to_core(up, half[0], 0)

    def when_push(cond, src, dst, send, recv, to):
        @pl.when(cond)
        def _():
            push(src, dst, send, recv, to)

    lo, hi = pl.ds(0, ROWS), pl.ds(ROWS, ROWS)
    above, below = near(0, 0, 1, 0), near(0, 0, 3, 0)
    to_above, to_below = lax.div(lax.rem(z + 1, 4), 2), lax.div(lax.rem(z + 3, 4), 2)

    def same_side(r):
        return lax.div(lax.rem(x + r, 4), 2) == lax.rem(z, 2)

    def product(tl, r, blocks):
        acc = None
        for hh in range(2):
            right = jnp.concatenate([wbuf[r, 2 * hh], wbuf[r, 2 * hh + 1]], axis=1)
            part = jnp.dot(blocks(2 * hh + (low if tl == 0 else 1 - low)), right, preferred_element_type=F32)
            acc = part if acc is None else acc + part
        return acc

    def half_copy(tl, r, cc):
        rows = pl.ds(pl.multiple_of(cc * ROWS, ROWS), ROWS)
        return remote(
            cstage.at[tl, r, 1 - lax.div(z, 2), rows], zh.at[tl, r, cc], zh_s, zh_r.at[tl, r, cc],
            near(0, 0, 1 + 2 * cc, 0),
        )

    def tasks(tl, turns, ready=None):
        @pl.loop(0, 2)
        def _(i):
            cc = lax.rem(core + i, 2)

            if ready is not None:

                @pl.when(i == 1)
                def _():
                    ready()

            for r in turns:
                acc = product(tl, r, lambda block: abuf[block, cc])
                rows = pl.ds(pl.multiple_of(cc * ROWS, ROWS), ROWS)
                cstage[tl, r, 0, rows, :] = acc[:, :LANES].astype(BF16)
                cstage[tl, r, 1, rows, :] = acc[:, LANES:].astype(BF16)

                @pl.when(same_side(r))
                def _():
                    half_copy(tl, r, cc).start()

    def add_on(tl, r):
        other_side = jnp.logical_not(same_side(r))
        e = lax.rem(lax.rem(x + r, 4), 2)

        @pl.when(other_side)
        def _():
            arrived(zh.at[tl, r, 0], zh_r.at[tl, r, 0])
            mine = cstage[tl, r, to_above, lo, :].astype(F32)
            cstage[tl, r, to_above, lo, :] = (mine + zh[tl, r, 0].astype(F32)).astype(BF16)

        when_push(
            other_side, cstage.at[tl, r, to_above], zbuf.at[0, tl, e], zs_s, zs_r.at[0, tl, e], above
        )

        @pl.when(other_side)
        def _():
            arrived(zh.at[tl, r, 1], zh_r.at[tl, r, 1])
            mine = cstage[tl, r, to_below, hi, :].astype(F32)
            cstage[tl, r, to_below, hi, :] = (mine + zh[tl, r, 1].astype(F32)).astype(BF16)

        when_push(
            other_side, cstage.at[tl, r, to_below], zbuf.at[1, tl, e], zs_s, zs_r.at[1, tl, e], below
        )

    def near_ready():
        arrived(feat, cf_r.at[0])

    tasks(1, (0,), near_ready)
    pass_on(3)
    tasks(1, (1,))
    add_on(1, 0)
    tasks(1, (3,))
    arrived(abuf.at[far, core, half[0]], ar_r.at[0])
    to_core(far, half[0], 1)
    arrived(abuf.at[far, core, half[1]], ar_r.at[1])
    to_core(far, half[1], 1)
    pltpu.make_async_copy(kp, kp, load_sem.at[11]).wait()
    for dy in range(4):
        for dc in range(2):
            if dy or dc:
                push(kp.at[dy, dc], kz.at[high, low, core], k_s, k_r.at[0], near(0, dy, 0, dc))

    for g, to in ((1, other), (2, partner), (3, across)):
        push(se_part.at[g], se_pin.at[g], sp_s, sp_r.at[0], to)

    def far_ready():
        arrived(abuf.at[far, 1 - core], cf_r.at[1])

    tasks(0, (0,), far_ready)
    add_on(1, 1)
    tasks(0, (1,))
    add_on(1, 3)
    tasks(0, (3,))

    arrived(wbuf.at[2], rl_r.at[0])
    tasks(1, (2,))
    tasks(0, (2,))
    for add_tl, add_r in ((0, 0), (0, 1), (0, 3), (1, 2), (0, 2)):
        add_on(add_tl, add_r)

    arrived(abuf.at[0, 0, pl.ds(0, 224)], k_r.at[0])

    own_x = lax.rem(z, 2) * 2
    first_e = jnp.where(lax.rem(own_x - x + 4, 4) == 2, 1, 0)
    for e in (first_e, 1 - first_e):
        for tl in (1, 0):
            token_low = low if tl == 0 else 1 - low
            total = cstage[tl, lax.rem(own_x + e - x + 4, 4), lax.div(z, 2)].astype(F32)
            for way in range(2):
                arrived(zbuf.at[way, tl, e], zs_r.at[way, tl, e])
                total = total + zbuf[way, tl, e].astype(F32)
            total = total.astype(BF16).astype(F32)
            for cc in range(2):
                rows = slice(cc * ROWS, (cc + 1) * ROWS)
                value = kz[e, token_low, cc].astype(F32) * total[rows]
                red[e, token_low, pl.ds(cc * ROWS, ROWS), :] = value.astype(BF16)
            for pc in range(2):
                py = 2 * e + token_low
                dy, dc = lax.rem(py - y + 4, 4), lax.rem(pc - core + 2, 2)
                src = red.at[e, token_low, pl.ds(pc * ROWS, ROWS)]
                dst = xh.at[core * 4 + y, pl.ds(SPAN, ROWS)]
                when_push(dy + dc > 0, src, dst, fs_s, fs_r.at[0], device(x, py, z, pc))

                @pl.when(dy + dc == 0)
                def _():
                    xh[core * 4 + y, pl.ds(SPAN, ROWS), :] = red[e, token_low, pl.ds(pc * ROWS, ROWS), :]

            right = red[e, token_low]
            lanes = pl.ds(pl.multiple_of(token_low * 2 * ROWS, 2 * ROWS), 2 * ROWS)
            for r in (1, 3, 2, 0):
                left = pick[pl.ds(r * 4, 4), :, lanes].reshape(4 * SPAN, 2 * ROWS)
                some = jnp.dot(left, right, preferred_element_type=F32)
                if tl == 1:
                    slot_half[r] = some
                    continue
                slot[e, r] = (slot_half[r] + some).astype(BF16)
                if r:
                    push(slot.at[e, r], slot_in.at[e, r], st_s, st_r.at[e], near(r, 0, 0, 0))

    for e in range(2):
        for token_low in range(2):
            for pc in range(2):
                py = 2 * e + token_low
                last = red.at[e, token_low, pl.ds(pc * ROWS + SPAN, SPAN)]
                edge = xh.at[core * 4 + y, pl.ds(0, SPAN)]
                if pc == 0:
                    following = device(x, py, z, 1)
                    away = (py != y) | (core == 0)
                else:
                    wrap = lax.div(x, 3)
                    next_low = token_low + wrap - 2 * token_low * wrap
                    following = device(lax.rem(x + 1, 4), 2 * e + next_low, z, 0)
                    away = core >= 0
                at = token_low * 2 + pc
                when_push(away, last, edge, hs_s, hs_r.at[0], following)
                if pc == 0:

                    @pl.when(jnp.logical_not(away))
                    def _():
                        xh[core * 4 + y, pl.ds(0, SPAN), :] = red[e, token_low, pl.ds(SPAN, SPAN), :]

    arrived(se_pin.at[pl.ds(1, 3)], sp_r.at[0])
    se_sum = se_part[0].astype(F32) + se_pin[1].astype(F32) + se_pin[2].astype(F32) + se_pin[3].astype(F32)
    for r in range(4):
        rows = se_sum[8 * r : 8 * r + 8]
        se_slot[r] = jnp.concatenate([rows, jnp.zeros_like(rows)], axis=0).astype(BF16)
        if r:
            push(se_slot.at[r], se_sin.at[r], sq_s, sq_r.at[0], near(r, 0, 0, 0))

    arrived(abuf.at[0, 0, pl.ds(0, 224)], fs_r.at[0])
    gate_load.wait()

    def convolve(b):
        @pl.loop(0, WIDTH // LANES)
        def _(p):
            lanes = column(p)
            left = toep[b, pl.ds(p * 8, 8)].reshape(8 * SPAN, 2 * SPAN)
            big[...] = jnp.dot(left, xh[p, pl.ds(b * SPAN, 2 * SPAN), :], preferred_element_type=F32)
            group = lax.div(iota((SPAN, LANES), 1), 16)
            out = big[pl.ds(0, SPAN), :]
            for g in range(1, 8):
                out = jnp.where(group == g, big[pl.ds(g * SPAN, SPAN), :], out)
            rows = pl.ds(b * SPAN, SPAN)
            mixed[rows, lanes] = (gate[rows, lanes].astype(F32) * out).astype(BF16)

    convolve(1)
    upper, lower = pl.ds(0, SPAN), pl.ds(SPAN, SPAN)
    stores = [load(mixed.at[lower], mixed_out.at[lower], 12)]

    def states(e):
        arrived(abuf.at[0, 0, pl.ds(0, 192)], st_r.at[e])
        slot_sum[e] = (
            slot[e, 0].astype(F32) + slot_in[e, 1].astype(F32) + slot_in[e, 2].astype(F32) + slot_in[e, 3].astype(F32)
        ).astype(BF16)
        for pl_, pc in ((0, 0), (0, 1), (1, 0), (1, 1)):
            py = 2 * e + pl_
            dy, dc = lax.rem(py - y + 4, 4), lax.rem(pc - core + 2, 2)
            rows = pl.ds((pl_ * 2 + pc) * SPAN, SPAN)
            when_push(
                dy + dc > 0, slot_sum.at[e, rows], st.at[core * 4 + y], sy_s, sy_r.at[0],
                device(x, py, z, pc),
            )

            @pl.when(dy + dc == 0)
            def _():
                st[core * 4 + y] = slot_sum[e, rows, :]

    states(first_e)
    states(1 - first_e)
    for at_core, count in ((0, 128), (1, 112)):

        @pl.when(core == at_core)
        def _():
            arrived(abuf.at[0, 0, pl.ds(0, count)], hs_r.at[0])

    convolve(0)
    stores.append(load(mixed.at[upper], mixed_out.at[upper], 13))

    arrived(se_sin.at[pl.ds(1, 3)], sq_r.at[0])
    se_total = se_slot[0].astype(F32)
    for r in (1, 2, 3):
        se_total = se_total + se_sin[r].astype(F32)
    se_state[...] = se_total.astype(BF16)
    stores.append(load(se_state, se_out.at[0], 14))
    arrived(abuf.at[0, 0, pl.ds(0, 112)], sy_r.at[0])
    for p in range(8):
        mr_state[:, pl.ds(p * LANES, LANES)] = st[p]
    stores.append(load(mr_state, mr_out.at[0], 15))

    block = abuf.at[0, 0]
    for sem, ref in (
        (halo_s, halo), (ws_s, wq), (xs_s, wbuf.at[pl.ds(0, 2)]), (rl_s, wbuf.at[0]), (as_s, abuf.at[0]),
        (ar_s, block), (cf_s, abuf.at[pl.ds(0, 2)]), (k_s, block.at[pl.ds(0, 224)]), (zh_s, kp),
        (zs_s, cstage.at[0]), (fs_s, block.at[pl.ds(0, 224)]), (st_s, wbuf.at[0, pl.ds(0, 3)]),
        (sy_s, block.at[pl.ds(0, 112)]), (sp_s, block.at[pl.ds(0, 96)]), (sq_s, block.at[pl.ds(0, 48)]),
    ):
        remote(ref, ref, sem, sem, other).wait_send()
    for at_core, count in ((0, 128), (1, 112)):

        @pl.when(core == at_core)
        def _():
            ref = block.at[pl.ds(0, count)]
            remote(ref, ref, hs_s, hs_s, other).wait_send()

    for copy in stores:
        copy.wait()


def finish(mixed_in, se_in, mr_in, mixed, se_state, mr_state):
    mixed[...] = mixed_in[...]
    se_state[...] = se_in[:, pl.ds(0, TAPS - 1), :]
    mr_state[...] = mr_in[:, pl.ds(0, SPAN - 1), :]


def on_device(feats_se, filt_se, w_out, feats_mr, filt_mr, lengths, owners):
    vmem, anywhere = pl.BlockSpec(memory_space=pltpu.VMEM), pl.BlockSpec(memory_space=pl.ANY)
    dma = pltpu.SemaphoreType.DMA
    scratch = [
        pltpu.SMEM((8,), I32), pltpu.SMEM((8,), I32),
        pltpu.VMEM((TAPS, 64), F32), pltpu.VMEM((64, SPAN), F32),
        pltpu.VMEM((ROWS, WIDTH), BF16), pltpu.VMEM((16, WIDTH), BF16), pltpu.VMEM((SPAN, WIDTH), BF16),
        pltpu.VMEM((3, ROWS, WIDTH), BF16),
        pltpu.VMEM((2, 16, WIDTH), BF16),
        pltpu.VMEM((ROWS, WIDTH), BF16),
        pltpu.VMEM((4, 2, ROWS, LANES), BF16),
        pltpu.VMEM((2, 2, 2, ROWS, LANES), BF16),
        pltpu.VMEM((ROWS + 16, WIDTH), F32),
        pltpu.VMEM((ROWS, LANES), I32),
        pltpu.VMEM((3, WIDTH, LANES), BF16),
        pltpu.VMEM((4, 4, WIDTH, LANES), BF16),
        pltpu.VMEM((4, 2, ROWS, WIDTH), BF16),
        pltpu.VMEM((2, 4, 2, 2 * ROWS, LANES), BF16),
        pltpu.VMEM((2, 4, 2, ROWS, LANES), BF16),
        pltpu.VMEM((2, 2, 2, 2 * ROWS, LANES), BF16),
        pltpu.VMEM((2, 2, 2 * ROWS, LANES), BF16),
        pltpu.VMEM((64, SPAN), F32),
        pltpu.VMEM((2, 64, SPAN, 2 * SPAN), BF16),
        pltpu.VMEM((16, SPAN, 4 * ROWS), BF16),
        pltpu.VMEM((8, ROWS + SPAN, LANES), BF16),
        pltpu.VMEM((4, 4 * SPAN, LANES), F32),
        pltpu.VMEM((2, 4, 4 * SPAN, LANES), BF16),
        pltpu.VMEM((2, 4, 4 * SPAN, LANES), BF16),
        pltpu.VMEM((2, 4 * SPAN, LANES), BF16),
        pltpu.VMEM((8, SPAN, LANES), BF16),
        pltpu.VMEM((ROWS, WIDTH), BF16),
        pltpu.VMEM((4, 32, WIDTH), BF16),
        pltpu.VMEM((4, 32, WIDTH), BF16),
        pltpu.VMEM((4, 16, WIDTH), BF16),
        pltpu.VMEM((4, 16, WIDTH), BF16),
        pltpu.VMEM((8 * SPAN, LANES), F32),
        pltpu.VMEM((8, WIDTH), F32),
        dma((16,)), dma((16,)), dma((1,)), dma((3,)), dma((2, 4)), dma((1,)), dma((2, 2)), dma((2,)), dma((2,)),
        dma((1,)), dma((2, 4, 2)), dma((2, 2, 2)), dma((1,)), dma((1,)), dma((2,)), dma((1,)), dma((1,)), dma((1,)),
    ]
    results = pl.pallas_call(
        kernel,
        out_shape=(
            jax.ShapeDtypeStruct((ROWS, WIDTH), BF16),
            jax.ShapeDtypeStruct((1, 16, WIDTH), BF16),
            jax.ShapeDtypeStruct((1, SPAN, WIDTH), BF16),
        ),
        in_specs=[anywhere] * 7,
        out_specs=(anywhere, anywhere, anywhere),
        scratch_shapes=scratch,
        compiler_params=pltpu.CompilerParams(
            collective_id=0, has_side_effects=True, vmem_limit_bytes=56 * 2**20
        ),
        cost_estimate=pl.CostEstimate(flops=5 * 10**9, bytes_accessed=5 * 10**6, transcendentals=0),
        name="hyena",
    )(lengths, owners, filt_se.T, filt_mr, feats_se, w_out, feats_mr)
    return pl.pallas_call(
        finish,
        out_shape=(
            jax.ShapeDtypeStruct((ROWS, WIDTH), BF16),
            jax.ShapeDtypeStruct((1, TAPS - 1, WIDTH), BF16),
            jax.ShapeDtypeStruct((1, SPAN - 1, WIDTH), BF16),
        ),
        in_specs=[vmem] * 3,
        out_specs=(vmem, vmem, vmem),
        compiler_params=pltpu.CompilerParams(vmem_limit_bytes=56 * 2**20),
        name="outputs",
    )(*results)


def solution(mesh):
    in_specs = (
        P(None, "ctx", "chan"),
        P("chan", None),
        P("chan", "ctx"),
        P(None, "ctx", "chan"),
        P("chan", None),
        P(),
        P(),
    )
    out_specs = (P("ctx", "chan"), P("ctx", None, "chan"), P("ctx", None, "chan"))
    return jax.shard_map(
        on_device, mesh=mesh, in_specs=in_specs, out_specs=out_specs, check_vma=False
    )
```
